128 devices in a mesh: dp: 32 (over y, x, core), mp: 4 (over z).
Axes of the slice: x: 4, y: 4, z: 4, core: 2. Of those that a mesh axis runs over, the one named last changes fastest.
Arguments:
- gradient: bfloat16 [8, 1024, 28672], P(None, 'dp', 'mp')
- second_moment: bfloat16 [8, 1024, 28672], P(None, 'dp', 'mp'), as said below
- owner_table: int32 [56, 1], replicated, may hold values from 0 to 31; in each aligned block of 56 rows (0 to 55, 56 to 111, ...) at most 3 rows name the same one
- left_roots: bfloat16 [32, 4, 3, 1024, 1024], P('dp', 'mp'), as said below
- right_roots: bfloat16 [32, 4, 3, 1024, 1024], P('dp', 'mp'), as said below
Outputs:
- update: bfloat16 [8, 1024, 28672], P(None, 'dp', 'mp')
The draws below stay inside these ranges and needn't reach their ends.
Inputs may be any that keep to these rules, and one draw needn't show every extreme that they name: `owner_table`: no index of dp owns more than 3 blocks, some owns exactly 3, and every index owns at least one. `left_roots`: every entry has magnitude below five; no structure is promised. `right_roots`: every entry has magnitude below five; no structure is promised. `second_moment`: Positive.
All inputs are finite; a program needn't handle non-finite values.
Results may differ from the reference program's by a relative error of at most 0.005.
Values may be sent and summed in bfloat16 or wider, within the bound.
No kernel may reach another device: no remote copies, remote signals or barrier semaphores. Data moves between devices by JAX's collectives and lax.ppermute only.
A program may use at most 128 MiB of HBM per device.

```python
import math
import jax
import jax.numpy as jnp
import numpy as np
from jax import lax

FF = 28672
BLK = 1024
NBR = 8
CB = 7
NBLK = 56
CAP = 3
N_DP = 32
N_MP = 4


def loguniform_draw(key, shape, low, high):
    return jnp.exp(jax.random.uniform(key, shape, jnp.float32, math.log(low), math.log(high)))


def draw_gradient(key, part):
    key = jax.random.fold_in(key, 11)
    key_row, key_col, key_base = jax.random.split(key, 3)
    row_scale = loguniform_draw(key_row, (NBR, BLK, 1), 0.3, 3.3)
    col_scale = loguniform_draw(key_col, (1, 1, FF), 0.3, 3.3)
    ramp = jnp.exp(math.log(3.0) * jnp.arange(BLK, dtype=jnp.float32) / BLK).reshape(1, BLK, 1)
    base = jax.random.normal(key_base, (NBR, BLK, FF), jnp.float32)
    return (0.5 * base * row_scale * col_scale * ramp).astype(jnp.bfloat16)


def draw_second_moment(key, part):
    key = jax.random.fold_in(key, 12)
    key_level, key_entry = jax.random.split(key, 2)
    level = loguniform_draw(key_level, (NBR, 1, FF // BLK), 0.1, 10.0)
    level = jnp.repeat(level, BLK, axis=2)
    entries = loguniform_draw(key_entry, (NBR, BLK, FF), 0.5, 2.0)
    return (level * entries).astype(jnp.bfloat16)


def root_shape():
    return (N_DP, N_MP, CAP, BLK, BLK)


def identity_mask():
    index_rows = jnp.arange(BLK)[:, None]
    index_cols = jnp.arange(BLK)[None, :]
    return index_rows == index_cols


def draw_left_roots(key, part):
    key = jax.random.fold_in(key, 13)
    key_diag, key_noise = jax.random.split(key, 2)
    diagonal = loguniform_draw(key_diag, (N_DP, N_MP, CAP, 1, BLK), 0.5, 2.0)
    noise = 0.4 * jax.random.normal(key_noise, root_shape(), jnp.float32) / math.sqrt(BLK)
    return (jnp.where(identity_mask(), diagonal, 0.0) + noise).astype(jnp.bfloat16)


def draw_right_roots(key, part):
    key = jax.random.fold_in(key, 14)
    key_diag, key_noise = jax.random.split(key, 2)
    diagonal = loguniform_draw(key_diag, (N_DP, N_MP, CAP, 1, BLK), 0.5, 2.0)
    noise = 0.4 * jax.random.normal(key_noise, root_shape(), jnp.float32) / math.sqrt(BLK)
    return (jnp.where(identity_mask(), diagonal, 0.0) + noise).astype(jnp.bfloat16)


def assign_block(key, own, number, rows, count, top, most, lean):
    ranking = jax.random.permutation(key, count)
    crowded, ordinary = shares(count, rows * top, most, lean, True), shares(count, rows * top, most, lean, False)
    places = jnp.arange(count)

    def named(lengths, offset_by):
        used = int((lengths > 0).sum())
        fixed = max(1, used // 4)
        passed = fixed + (places - fixed + offset_by * (used - fixed)) % max(1, count - fixed)
        return jnp.zeros((count,), jnp.int32).at[ranking[jnp.where(places < fixed, places, passed)]].set(jnp.asarray(lengths, jnp.int32))

    lengths = jnp.where(number % 4 == 0, named(crowded, number // 4), named(ordinary, number - number // 4 - 1))
    mixed = jax.random.permutation(jax.random.fold_in(own, 3), count)
    source_of, sink = mixed[0:count // 2 * 2:2], mixed[1:count // 2 * 2:2]
    room = jnp.minimum(lengths[source_of] - 1, most - lengths[sink]) // 2
    room = jnp.where((source_of == ranking[0]) | (sink == ranking[0]) | (lengths[sink] == 0), 0, jnp.maximum(room, 0))
    passed = jax.random.randint(jax.random.fold_in(own, 4), (count // 2,), 0, 1 << 20) % (room + 1)
    lengths = lengths.at[source_of].add(-passed).at[sink].add(passed)
    items = jnp.searchsorted(jnp.cumsum(lengths), jnp.arange(rows * top), side="right").astype(jnp.int32)
    table = items.reshape(top, rows).T
    table = table[jax.random.permutation(jax.random.fold_in(own, 1), rows)]
    offset_by = jax.random.randint(jax.random.fold_in(own, 2), (rows, 1), 0, top)
    return jnp.take_along_axis(table, (jnp.arange(top)[None, :] + offset_by) % top, axis=1)


def shares(amount, total, reach, slope, full):
    portions = [(1 << 20) // math.isqrt(grade ** slope) + 1 for grade in range(1, amount + 1)]
    largest = reach if full else min(reach, max(-(-total // amount), total * portions[0] // sum(portions)))
    least = 1 if total - largest >= amount - 1 else 0
    counts, surplus = [largest] + [least] * (amount - 1), total - largest - least * (amount - 1)
    while surplus > 0:
        free = [i for i in range(1, amount) if counts[i] < largest] or [i for i in range(1, amount) if counts[i] < reach]
        mass, remaining = sum([portions[i] for i in free]), surplus
        for i in free:
            more = min(reach - counts[i], max(1, remaining * portions[i] // mass), surplus)
            counts[i] = counts[i] + more
            surplus = surplus - more
    return np.array(counts)


def setup_inputs(seed: int = 0) -> dict:
    arg_keys = jax.random.split(jax.random.key(seed), 6)
    gradient = draw_gradient(jax.random.fold_in(arg_keys[5], 71), 0)
    second_moment = draw_second_moment(jax.random.fold_in(arg_keys[5], 71), 0)
    owner_table_keys = jax.random.split(jax.random.fold_in(arg_keys[2], 1), NBLK // NBLK)
    owner_table_turns = jax.random.permutation(jax.random.fold_in(arg_keys[2], 3), NBLK // NBLK)
    owner_table = jax.vmap(lambda own, number: assign_block(jax.random.fold_in(arg_keys[2], 2), own, number, NBLK, N_DP, 1, CAP, 2))(owner_table_keys, owner_table_turns).reshape((NBLK, 1))
    left_roots = draw_left_roots(jax.random.fold_in(arg_keys[5], 71), 0)
    right_roots = draw_right_roots(jax.random.fold_in(arg_keys[5], 71), 0)
    return dict(gradient=gradient, second_moment=second_moment, owner_table=owner_table, left_roots=left_roots, right_roots=right_roots)


beta_two = 0.95
eps_adam = 1e-08
eps_norm = 1e-06

def slot_numbers(owners):
    total_count = owners.shape[0]
    row_ids = lax.broadcasted_iota(jnp.int32, (total_count, total_count), 0)
    others = lax.broadcasted_iota(jnp.int32, (total_count, total_count), 1)
    earlier = (owners[:, None] == owners[None, :]) & (others < row_ids)
    return lax.optimization_barrier(jnp.sum(earlier.astype(jnp.int32), axis=1)).astype(jnp.int32)

def reference(gradient, second_moment, owner_table, left_roots, right_roots):
    owners = owner_table[:, 0].astype(jnp.int32)
    slots = slot_numbers(owners)
    zero_index = jnp.zeros((), jnp.int32)

    def one_block(index):
        group = (index // NBLK).astype(jnp.int32)
        within = (index % NBLK).astype(jnp.int32)
        row_block = (within // CB).astype(jnp.int32)
        col_start = ((group * CB + within % CB) * BLK).astype(jnp.int32)
        starts = (row_block, zero_index, col_start)
        piece = lax.dynamic_slice(gradient, starts, (1, BLK, BLK))[0]
        moment_piece = lax.dynamic_slice(second_moment, starts, (1, BLK, BLK))[0]
        grad_wide = piece.astype(jnp.float32)
        moment = beta_two * moment_piece.astype(jnp.float32) + (1.0 - beta_two) * grad_wide * grad_wide
        adam_dir = grad_wide / (jnp.sqrt(moment) + eps_adam)
        rms_adam = jnp.sqrt(jnp.mean(adam_dir * adam_dir) + eps_norm)
        left_root = left_roots[owners[within], group, slots[within]]
        right_root = right_roots[owners[within], group, slots[within]]
        left_times = jnp.dot(left_root, piece, preferred_element_type=jnp.float32).astype(jnp.bfloat16)
        product = jnp.dot(left_times, right_root, preferred_element_type=jnp.float32)
        rms_shampoo = jnp.sqrt(jnp.mean(product * product) + eps_norm)
        return (product * (rms_adam / rms_shampoo)).astype(jnp.bfloat16)
    blocks = lax.map(one_block, jnp.arange(N_MP * NBLK, dtype=jnp.int32))
    blocks = blocks.reshape(N_MP, NBR, CB, BLK, BLK).transpose(1, 3, 0, 2, 4)
    return blocks.reshape(NBR, BLK, FF)
```

```python
import functools

import jax
import jax.numpy as jnp
from jax import lax
from jax.experimental import pallas as pl
from jax.experimental.pallas import tpu as pltpu
from jax.sharding import PartitionSpec as P

beta_two = 0.95
eps_adam = 1e-08
eps_norm = 1e-06

TILE = 256
LANES = 128
SUBLANES = 16
IN_HBM = pl.BlockSpec(memory_space=pltpu.HBM)
IN_VMEM = pl.BlockSpec(memory_space=pltpu.VMEM)
IN_SMEM = pl.BlockSpec(memory_space=pltpu.SMEM)


def slot_numbers(owners):
    total_count = owners.shape[0]
    row_ids = lax.broadcasted_iota(jnp.int32, (total_count, total_count), 0)
    others = lax.broadcasted_iota(jnp.int32, (total_count, total_count), 1)
    earlier = (owners[:, None] == owners[None, :]) & (others < row_ids)
    return jnp.sum(earlier.astype(jnp.int32), axis=1)


def pack_kernel(full_slots, owner_ref, grad_ref, send_ref, counts, sems):
    block_rows, row_count, width = grad_ref.shape
    block_size = send_ref.shape[2]
    block_cols = width // block_size
    half = row_count // 2

    def clear(index, carry):
        counts[index] = 0
        return carry

    lax.fori_loop(0, send_ref.shape[0], clear, 0, unroll=8)
    waits = []
    for r in range(block_rows):
        for c in range(block_cols):
            b = r * block_cols + c
            owner = owner_ref[b]
            slot = counts[owner]
            counts[owner] = slot + 1
            columns = pl.ds(c * block_size, block_size)

            @pl.when(slot < full_slots)
            def _():
                start = pl.multiple_of(slot * row_count, row_count)
                pltpu.make_async_copy(
                    grad_ref.at[r, :, columns],
                    send_ref.at[owner, pl.ds(start, row_count), :],
                    sems.at[b],
                ).start()

            if full_slots * row_count < send_ref.shape[1]:
                @pl.when(slot >= full_slots)
                def _():
                    first = 2 * lax.div(owner, 2)
                    for h in range(2):
                        pltpu.make_async_copy(
                            grad_ref.at[r, pl.ds(h * half, half), columns],
                            send_ref.at[first + h, pl.ds(full_slots * row_count, half), :],
                            sems.at[b],
                        ).start()

            waits.append(
                pltpu.make_async_copy(
                    grad_ref.at[r, :, columns], send_ref.at[0, pl.ds(0, row_count), :], sems.at[b]
                )
            )
    for wait in waits:
        wait.wait()


def pack(owners, gradient, group_size, rows, full_slots, block_size):
    return pl.pallas_call(
        functools.partial(pack_kernel, full_slots),
        out_shape=jax.ShapeDtypeStruct((group_size, rows, block_size), jnp.bfloat16),
        in_specs=[IN_SMEM, IN_HBM],
        out_specs=IN_HBM,
        scratch_shapes=[
            pltpu.SMEM((group_size,), jnp.int32),
            pltpu.SemaphoreType.DMA((owners.shape[0],)),
        ],
        compiler_params=pltpu.CompilerParams(vmem_limit_bytes=16 * 2**20),
        cost_estimate=pl.CostEstimate(flops=0, bytes_accessed=4 * gradient.size, transcendentals=0),
    )(owners, gradient)


def three_parts(value):
    high = value.astype(jnp.bfloat16)
    rest = value - high.astype(jnp.float32)
    middle = rest.astype(jnp.bfloat16)
    low = (rest - middle.astype(jnp.float32)).astype(jnp.bfloat16)
    return high, middle, low


def extra_tile(sums, squares):
    rows = lax.broadcasted_iota(jnp.int32, (SUBLANES, LANES), 0)
    content = jnp.zeros((SUBLANES, LANES), jnp.float32)
    for i, part in enumerate([*three_parts(sums), *three_parts(squares)]):
        content = jnp.where(rows == i, part.astype(jnp.float32), content)
    return content.astype(jnp.bfloat16)


def block_product(left_rows, grad, right, times, put):
    count = times.shape[0] // TILE
    for m in range(count):
        times[m * TILE : (m + 1) * TILE, :] = jnp.dot(
            left_rows(m), grad, preferred_element_type=jnp.float32
        ).astype(jnp.bfloat16)
    total = jnp.zeros((8, grad.shape[1]), jnp.float32)
    for m in range(count):
        value = jnp.dot(
            times[m * TILE : (m + 1) * TILE, :], right, preferred_element_type=jnp.float32
        )
        total = total + jnp.sum((value * value).reshape(TILE // 8, 8, -1), axis=0)
        put(m, value.astype(jnp.bfloat16))
    return jnp.sum(jnp.sum(total, axis=0, keepdims=True), axis=1, keepdims=True)


def multiply_kernel(
    slot_count, final, mine_ref, sums_ref, recv_ref, left_ref, right_ref, out_ref, squares_ref,
    grad, times, product, extra, grad_sems, out_sems, extra_sem,
):
    _, group_size, row_count, block_size = grad.shape
    tile_count = block_size // TILE
    per_tile = TILE // row_count
    slot_tiles = product.shape[2]
    lane_tiles = block_size // LANES

    def load(s):
        return pltpu.make_async_copy(
            recv_ref.at[:, pl.ds(s * row_count, row_count), :], grad.at[s], grad_sems.at[s]
        )

    def store(s, m):
        return pltpu.make_async_copy(
            product.at[s, pl.ds(m * per_tile, per_tile)],
            out_ref.at[pl.ds(m * per_tile, per_tile), pl.ds(s * slot_tiles, slot_tiles)],
            out_sems.at[s, m],
        )

    for s in range(slot_count):
        @pl.when(mine_ref[s] >= 0)
        def _():
            load(s).start()

    lane = lax.broadcasted_iota(jnp.int32, (1, LANES), 1)
    squares = jnp.zeros((1, LANES), jnp.float32)
    for s in range(slot_count):
        def compute(s=s):
            load(s).wait()

            def put(m, tile):
                for j in range(lane_tiles):
                    part = tile[:, j * LANES : (j + 1) * LANES].reshape(
                        per_tile, row_count // SUBLANES, SUBLANES, LANES
                    )
                    for h in range(row_count // SUBLANES):
                        product[s, m * per_tile : (m + 1) * per_tile, h * lane_tiles + j] = part[:, h]
                store(s, m).start()

            return block_product(
                lambda m: left_ref[s, m * TILE : (m + 1) * TILE, :],
                grad[s].reshape(block_size, block_size),
                right_ref[s],
                times,
                put,
            )

        value = lax.cond(mine_ref[s] >= 0, compute, lambda: jnp.zeros((1, 1), jnp.float32))
        squares = squares + jnp.where(lane == mine_ref[s], value, 0.0)
    squares_ref[...] = squares

    if final:
        extra[...] = jnp.broadcast_to(
            extra_tile(sums_ref[...], squares)[None, None], extra.shape
        )
        send_extra = pltpu.make_async_copy(
            extra, out_ref.at[:, pl.ds(out_ref.shape[1] - 1, 1)], extra_sem
        )
        send_extra.start()
    for s in range(slot_count):
        @pl.when(mine_ref[s] >= 0)
        def _():
            for m in range(tile_count):
                store(s, m).wait()
    if final:
        send_extra.wait()


def multiply(mine, sums, received, left_set, rights, slot_count, total_tiles, final):
    block_size = left_set.shape[-1]
    group_size = received.shape[0]
    row_count = block_size // group_size
    slot_tiles = row_count * block_size // (SUBLANES * LANES)
    return pl.pallas_call(
        functools.partial(multiply_kernel, slot_count, final),
        out_shape=(
            jax.ShapeDtypeStruct((group_size, total_tiles, SUBLANES, LANES), jnp.bfloat16),
            jax.ShapeDtypeStruct((1, LANES), jnp.float32),
        ),
        in_specs=[IN_SMEM, IN_VMEM, IN_HBM, IN_VMEM, IN_VMEM],
        out_specs=(IN_HBM, IN_VMEM),
        scratch_shapes=[
            pltpu.VMEM((slot_count, group_size, row_count, block_size), jnp.bfloat16),
            pltpu.VMEM((block_size, block_size), jnp.bfloat16),
            pltpu.VMEM((slot_count, group_size, slot_tiles, SUBLANES, LANES), jnp.bfloat16),
            pltpu.VMEM((group_size, 1, SUBLANES, LANES), jnp.bfloat16),
            pltpu.SemaphoreType.DMA((slot_count,)),
            pltpu.SemaphoreType.DMA((slot_count, block_size // TILE)),
            pltpu.SemaphoreType.DMA,
        ],
        compiler_params=pltpu.CompilerParams(vmem_limit_bytes=40 * 2**20),
        cost_estimate=pl.CostEstimate(
            flops=slot_count * 4 * block_size**3,
            bytes_accessed=slot_count * 8 * block_size**2,
            transcendentals=0,
        ),
    )(mine, sums, received, left_set, rights)


def shared_kernel(
    info_ref, sums_ref, squares_ref, own_ref, other_ref, left_ref, right_ref, before_ref, out_ref,
    grad, times, product, extra, grad_sems, out_sems, extra_sem,
):
    group_size, _, half, block_size = grad.shape
    tile_count = times.shape[0] // TILE
    per_tile = TILE // half
    lane_tiles = product.shape[1]
    first_tile = out_ref.shape[1] - 1 - lane_tiles
    block, core = info_ref[0], info_ref[1]
    del before_ref
    loads = [
        pltpu.make_async_copy(own_ref, grad.at[:, core], grad_sems.at[0]),
        pltpu.make_async_copy(other_ref, grad.at[:, 1 - core], grad_sems.at[1]),
    ]

    def store(m):
        return pltpu.make_async_copy(
            product.at[pl.ds(m * per_tile, per_tile)],
            out_ref.at[pl.ds(m * per_tile, per_tile), pl.ds(first_tile, lane_tiles)],
            out_sems.at[m],
        )

    def compute():
        for load in loads:
            load.start()
        for load in loads:
            load.wait()

        def put(m, tile):
            for j in range(lane_tiles):
                product[m * per_tile : (m + 1) * per_tile, j] = tile[
                    :, j * LANES : (j + 1) * LANES
                ].reshape(per_tile, SUBLANES, LANES)
            store(m).start()

        return block_product(
            lambda m: left_ref[m * per_tile : (m + 1) * per_tile].reshape(TILE, block_size),
            grad[...].reshape(block_size, block_size),
            right_ref[...],
            times,
            put,
        )

    value = lax.cond(block >= 0, compute, lambda: jnp.zeros((1, 1), jnp.float32))
    lane = lax.broadcasted_iota(jnp.int32, (1, LANES), 1)
    squares = squares_ref[...] + jnp.where(lane == block, value, 0.0)
    extra[...] = jnp.broadcast_to(extra_tile(sums_ref[...], squares)[None, None], extra.shape)
    send_extra = pltpu.make_async_copy(
        extra, out_ref.at[:, pl.ds(out_ref.shape[1] - 1, 1)], extra_sem
    )
    send_extra.start()

    @pl.when(block >= 0)
    def _():
        for m in range(tile_count):
            store(m).wait()

    send_extra.wait()


def multiply_shared(info, sums, squares, own, other, left_half, right, outgoing):
    group_size, half, block_size = own.shape
    lane_tiles = block_size // LANES
    rows = group_size * half
    return pl.pallas_call(
        shared_kernel,
        out_shape=jax.ShapeDtypeStruct(outgoing.shape, outgoing.dtype),
        in_specs=[IN_SMEM, IN_VMEM, IN_VMEM, IN_HBM, IN_HBM, IN_VMEM, IN_VMEM, IN_HBM],
        out_specs=IN_HBM,
        input_output_aliases={7: 0},
        scratch_shapes=[
            pltpu.VMEM((group_size, 2, half, block_size), jnp.bfloat16),
            pltpu.VMEM((rows, block_size), jnp.bfloat16),
            pltpu.VMEM((group_size, lane_tiles, SUBLANES, LANES), jnp.bfloat16),
            pltpu.VMEM((group_size, 1, SUBLANES, LANES), jnp.bfloat16),
            pltpu.SemaphoreType.DMA((2,)),
            pltpu.SemaphoreType.DMA((rows // TILE,)),
            pltpu.SemaphoreType.DMA,
        ],
        compiler_params=pltpu.CompilerParams(vmem_limit_bytes=32 * 2**20),
        cost_estimate=pl.CostEstimate(
            flops=4 * rows * block_size**2, bytes_accessed=8 * rows * block_size, transcendentals=0
        ),
    )(info, sums, squares, own, other, left_half, right, outgoing)


def unpack_kernel(full_slots, owner_ref, slot_ref, back_ref, out_ref, stage, out_sems):
    block_rows, row_count, width = stage.shape
    block_count = owner_ref.shape[0]
    block_cols = block_count // block_rows
    block_size = width // block_cols
    row_halves = row_count // SUBLANES
    lane_tiles = block_size // LANES
    last = back_ref.shape[1] - 1
    found = jnp.sum(back_ref[:, last].astype(jnp.float32), axis=0)
    count = float(block_size * block_size)
    rms_adam = jnp.sqrt((found[0:1] + found[1:2] + found[2:3]) / count + eps_norm)
    rms_shampoo = jnp.sqrt((found[3:4] + found[4:5] + found[5:6]) / count + eps_norm)
    scale = rms_adam / rms_shampoo
    writes = []
    for r in range(block_rows):
        for c in range(block_cols):
            b = r * block_cols + c
            factor = jnp.broadcast_to(scale[:, b : b + 1], (SUBLANES, LANES))
            owner, slot = owner_ref[b], slot_ref[b]
            for h in range(row_halves):
                whole = slot < full_slots
                source = jnp.where(whole, owner, 2 * lax.div(owner, 2) + h)
                first = jnp.where(
                    whole, (slot * row_halves + h) * lane_tiles, full_slots * row_halves * lane_tiles
                )
                for j in range(lane_tiles):
                    stage[
                        r,
                        h * SUBLANES : (h + 1) * SUBLANES,
                        c * block_size + j * LANES : c * block_size + (j + 1) * LANES,
                    ] = (back_ref[source, first + j].astype(jnp.float32) * factor).astype(jnp.bfloat16)
        write = pltpu.make_async_copy(stage.at[r], out_ref.at[r], out_sems.at[r])
        write.start()
        writes.append(write)
    for write in writes:
        write.wait()


def unpack(owners, slots, back, shape, full_slots):
    block_rows, row_count, width = shape
    return pl.pallas_call(
        functools.partial(unpack_kernel, full_slots),
        out_shape=jax.ShapeDtypeStruct(shape, jnp.bfloat16),
        in_specs=[IN_SMEM, IN_SMEM, IN_VMEM],
        out_specs=IN_HBM,
        scratch_shapes=[
            pltpu.VMEM(shape, jnp.bfloat16),
            pltpu.SemaphoreType.DMA((block_rows,)),
        ],
        compiler_params=pltpu.CompilerParams(vmem_limit_bytes=32 * 2**20),
        cost_estimate=pl.CostEstimate(
            flops=block_rows * row_count * width,
            bytes_accessed=4 * block_rows * row_count * width,
            transcendentals=0,
        ),
    )(owners, slots, back)


def adam_sums(gradient, second_moment, block_cols):
    block_rows, row_count, width = gradient.shape
    grad_wide = gradient.astype(jnp.float32)
    moment = beta_two * second_moment.astype(jnp.float32) + (1.0 - beta_two) * grad_wide * grad_wide
    adam_dir = grad_wide / (jnp.sqrt(moment) + eps_adam)
    sums = jnp.sum(
        (adam_dir * adam_dir).reshape(block_rows, row_count, block_cols, -1), axis=(1, 3)
    ).reshape(1, block_rows * block_cols)
    return jnp.pad(sums, ((0, 0), (0, LANES - block_rows * block_cols)))


def exchange(value):
    return lax.all_to_all(value, "dp", split_axis=0, concat_axis=0, tiled=True)


def on_device(gradient, second_moment, owner_table, left_roots, right_roots):
    group_size = lax.axis_size("dp")
    my_index = lax.axis_index("dp")
    _, row_count, width = gradient.shape
    block_size = left_roots.shape[-1]
    capacity = left_roots.shape[2]
    block_cols = width // block_size
    half = row_count // 2
    lane_tiles = block_size // LANES
    slot_tiles = lane_tiles * (row_count // SUBLANES)
    owners = owner_table[:, 0]
    slots = slot_numbers(owners)
    block_ids = jnp.arange(owners.shape[0], dtype=jnp.int32)
    last_slot = slots == capacity - 1
    both = last_slot[:, None] & last_slot[None, :] & ((owners[:, None] ^ 1) == owners[None, :])

    def mine_at(index, slot):
        return jnp.max(jnp.where((owners == index) & (slots == slot), block_ids, -1))

    def general(gradient, second_moment, left_roots, right_roots):
        send = pack(owners, gradient, group_size, capacity * row_count, capacity, block_size)
        received = exchange(send)
        mine = jnp.stack([mine_at(my_index, s) for s in range(capacity)])
        sums = adam_sums(gradient, second_moment, block_cols)
        outgoing, _ = multiply(
            mine, sums, received, left_roots[0, 0], right_roots[0, 0],
            capacity, capacity * slot_tiles + 1, True,
        )
        return unpack(owners, slots, exchange(outgoing), gradient.shape, capacity)

    def shared(gradient, second_moment, left_roots, right_roots):
        full = capacity - 1
        core = my_index & 1
        partner = [(i, i ^ 1) for i in range(group_size)]
        send = pack(owners, gradient, group_size, full * row_count + half, full, block_size)
        received = exchange(send)
        sums = adam_sums(gradient, second_moment, block_cols)
        mine = jnp.stack([mine_at(my_index, s) for s in range(full)])
        third, other_third = mine_at(my_index, full), mine_at(my_index ^ 1, full)
        info = jnp.stack([jnp.maximum(third, other_third), core])
        left_rows = left_roots[0, 0, full].reshape(group_size, 2, half, block_size)
        left_own = lax.dynamic_index_in_dim(left_rows, core, 1, keepdims=False)
        left_away = lax.dynamic_index_in_dim(left_rows, 1 - core, 1, keepdims=False)
        left_half = jnp.where(
            other_third >= 0, lax.ppermute(left_away, "dp", partner), left_own
        )
        right_own = right_roots[0, 0, full]
        right = jnp.where(other_third >= 0, lax.ppermute(right_own, "dp", partner), right_own)
        own = received[:, full * row_count :, :]
        other = lax.ppermute(own, "dp", partner)
        outgoing, squares = multiply(
            mine, sums, received, left_roots[0, 0], right_roots[0, 0],
            full, full * slot_tiles + lane_tiles + 1, False,
        )
        outgoing = multiply_shared(info, sums, squares, own, other, left_half, right, outgoing)
        return unpack(owners, slots, exchange(outgoing), gradient.shape, full)

    return lax.cond(
        jnp.any(both), general, shared, gradient, second_moment, left_roots, right_roots
    )


def solution(mesh):
    return jax.shard_map(
        on_device,
        mesh=mesh,
        in_specs=(
            P(None, "dp", "mp"),
            P(None, "dp", "mp"),
            P(),
            P("dp", "mp", None, None, None),
            P("dp", "mp", None, None, None),
        ),
        out_specs=P(None, "dp", "mp"),
        check_vma=False,
    )
```

```python
import functools

import jax
import jax.numpy as jnp
from jax import lax
from jax.experimental import pallas as pl
from jax.experimental.pallas import tpu as pltpu
from jax.sharding import PartitionSpec as P

beta_two = 0.95
eps_adam = 1e-08
eps_norm = 1e-06

TILE = 256
LANES = 128
SUBLANES = 16
IN_VMEM = pl.BlockSpec(memory_space=pltpu.VMEM)
IN_SMEM = pl.BlockSpec(memory_space=pltpu.SMEM)
IN_ANY = pl.BlockSpec(memory_space=pl.ANY)


def keep_hbm(*values):
    return [pltpu.with_memory_space_constraint(value, pltpu.HBM) for value in values]


def keep_vmem(*values):
    return [pltpu.with_memory_space_constraint(value, pltpu.VMEM) for value in values]


def pack_kernel(
    full_slots, capacity, first_pass, me_ref, owner_ref, grad_ref, moment_ref, left_ref, right_ref,
    send_ref, sums_ref, slot_ref, info_ref, conflict_ref, left_away, right_away,
    counts, table, stage, moments, partial, stage_sems, away_sems,
):
    block_rows, row_count, width = grad_ref.shape
    group_size, _, block_size = send_ref.shape
    block_cols = width // block_size
    half = row_count // 2
    pairs = [(grad_ref, stage)] + ([(moment_ref, moments)] if first_pass else [])
    loads = [
        [
            pltpu.make_async_copy(source.at[r], target.at[r], stage_sems.at[i, r])
            for i, (source, target) in enumerate(pairs)
        ]
        for r in range(block_rows)
    ]
    for row in loads:
        for load in row:
            load.start()
    me = me_ref[0]
    core = lax.rem(me, 2)
    if first_pass:
        away = [
            pltpu.make_async_copy(left_ref.at[capacity - 1, :, 1 - core], left_away, away_sems.at[0]),
            pltpu.make_async_copy(right_ref.at[capacity - 1], right_away, away_sems.at[1]),
        ]
        for copy in away:
            copy.start()

    for index in range(group_size):
        counts[index] = 0
        for slot in range(capacity):
            table[index * capacity + slot] = -1
    conflict_ref[0] = 0
    partial[...] = jnp.zeros(partial.shape, jnp.float32)

    def block(r, c):
        b = r * block_cols + c
        owner = owner_ref[b]
        slot = counts[owner]
        counts[owner] = slot + 1
        slot_ref[b] = slot
        columns = pl.ds(pl.multiple_of(c * block_size, block_size), block_size)
        shared = slot >= full_slots

        @pl.when(jnp.logical_not(shared))
        def _():
            start = pl.multiple_of(slot * row_count, row_count)
            send_ref[owner, pl.ds(start, row_count), :] = stage[r, :, columns]

        if full_slots < capacity:
            chip = lax.div(owner, 2)
            taken = table[(4 * chip + 1 - owner) * capacity + capacity - 1] >= 0

            @pl.when(shared & taken)
            def _():
                conflict_ref[0] = 1

            @pl.when(shared)
            def _():
                for h in range(2):
                    send_ref[2 * chip + h, pl.ds(full_slots * row_count, half), :] = stage[
                        r, pl.ds(h * half, half), columns
                    ]

        table[owner * capacity + slot] = b
        if first_pass:
            total = jnp.zeros((8, LANES), jnp.float32)
            for k in range(0, block_size, 2 * LANES):
                part = pl.ds(pl.multiple_of(c * block_size + k, 2 * LANES), 2 * LANES)
                wide = stage[r, :, part].astype(jnp.float32)
                moment = beta_two * moments[r, :, part].astype(jnp.float32) + (
                    (1.0 - beta_two) * wide * wide
                )
                direction = wide / (jnp.sqrt(moment) + eps_adam)
                value = jnp.sum((direction * direction).reshape(row_count // 8, 8, -1), axis=0)
                total = total + value[:, :LANES] + value[:, LANES:]
            partial[pl.ds(b, 1), :] = jnp.sum(total, axis=0, keepdims=True)

    for r in range(block_rows):
        for load in loads[r]:
            load.wait()
        lax.fori_loop(0, block_cols, lambda c, carry, r=r: (block(r, c), carry)[1], 0)

    for slot in range(capacity):
        info_ref[slot] = table[me * capacity + slot]
    info_ref[capacity] = table[(me + 1 - 2 * core) * capacity + capacity - 1]
    info_ref[capacity + 1] = core
    sums_ref[...] = lax.dot_general(
        jnp.ones((8, LANES), jnp.float32),
        partial[...],
        (((1,), (1,)), ((), ())),
        precision=lax.Precision.HIGHEST,
        preferred_element_type=jnp.float32,
    )[0:1]
    if first_pass:
        for copy in away:
            copy.wait()


def pack(me, owners, gradient, second_moment, left_set, rights, rows, full_slots):
    first_pass = second_moment is not None
    capacity, group_size, _, half, block_size = left_set.shape
    return pl.pallas_call(
        functools.partial(pack_kernel, full_slots, capacity, first_pass),
        out_shape=(
            pltpu.VMEM((group_size, rows, block_size), jnp.bfloat16),
            jax.ShapeDtypeStruct((1, LANES), jnp.float32),
            jax.ShapeDtypeStruct(owners.shape, jnp.int32),
            jax.ShapeDtypeStruct((capacity + 2,), jnp.int32),
            jax.ShapeDtypeStruct((1,), jnp.int32),
            pltpu.VMEM((group_size, half, block_size), jnp.bfloat16),
            pltpu.VMEM((block_size, block_size), jnp.bfloat16),
        ),
        in_specs=[IN_SMEM, IN_SMEM] + [IN_ANY] * 4,
        out_specs=(IN_VMEM, IN_VMEM, IN_SMEM, IN_SMEM, IN_SMEM, IN_VMEM, IN_VMEM),
        scratch_shapes=[
            pltpu.SMEM((group_size,), jnp.int32),
            pltpu.SMEM((group_size * capacity,), jnp.int32),
            pltpu.VMEM(gradient.shape, jnp.bfloat16),
            pltpu.VMEM(gradient.shape, jnp.bfloat16),
            pltpu.VMEM((LANES, LANES), jnp.float32),
            pltpu.SemaphoreType.DMA((2, gradient.shape[0])),
            pltpu.SemaphoreType.DMA((2,)),
        ],
        compiler_params=pltpu.CompilerParams(vmem_limit_bytes=24 * 2**20),
        cost_estimate=pl.CostEstimate(
            flops=10 * gradient.size, bytes_accessed=8 * gradient.size, transcendentals=2 * gradient.size
        ),
    )(
        me,
        owners,
        *keep_hbm(gradient, second_moment if first_pass else gradient, left_set, rights),
    )


def three_parts(value):
    high = value.astype(jnp.bfloat16)
    rest = value - high.astype(jnp.float32)
    middle = rest.astype(jnp.bfloat16)
    low = (rest - middle.astype(jnp.float32)).astype(jnp.bfloat16)
    return high, middle, low


def extra_tile(sums, squares):
    rows = lax.broadcasted_iota(jnp.int32, (SUBLANES, LANES), 0)
    content = jnp.zeros((SUBLANES, LANES), jnp.float32)
    for i, part in enumerate([*three_parts(sums), *three_parts(squares)]):
        content = jnp.where(rows == i, part.astype(jnp.float32), content)
    return content.astype(jnp.bfloat16)


def block_product(left_rows, grad, right_ready, right, times, put):
    count = times.shape[0] // TILE
    for m in range(count):
        times[m * TILE : (m + 1) * TILE, :] = jnp.dot(
            left_rows(m), grad(), preferred_element_type=jnp.float32
        ).astype(jnp.bfloat16)
    right_ready()
    total = jnp.zeros((8, times.shape[1]), jnp.float32)
    for m in range(count):
        value = jnp.dot(
            times[m * TILE : (m + 1) * TILE, :], right(), preferred_element_type=jnp.float32
        )
        total = total + jnp.sum((value * value).reshape(TILE // 8, 8, -1), axis=0)
        put(m, value.astype(jnp.bfloat16))
    return jnp.sum(jnp.sum(total, axis=0, keepdims=True), axis=1, keepdims=True)


def multiply_kernel(
    slot_count, final, info_ref, sums_ref, recv_ref, left_ref, right_ref,
    out_ref, squares_ref, left_half, right_third, left, right, times, left_sems, right_sems, third_sems,
):
    _, group_size, row_halves, _, block_size = left.shape
    row_count = row_halves * SUBLANES
    tile_count = block_size // TILE
    per_tile = TILE // row_count
    lane_tiles = block_size // LANES
    capacity = left_ref.shape[0]

    def left_load(s, m):
        rows = pl.ds(m * per_tile, per_tile)
        return pltpu.make_async_copy(left_ref.at[s, rows], left.at[s, rows], left_sems.at[s, m])

    def right_load(s):
        return pltpu.make_async_copy(right_ref.at[s], right.at[s], right_sems.at[s])

    for s in range(slot_count):
        @pl.when(info_ref[s] >= 0)
        def _():
            for m in range(tile_count):
                left_load(s, m).start()
            right_load(s).start()

    if not final:
        last = capacity - 1
        own, core = info_ref[last], info_ref[capacity + 1]

        def third_loads():
            return (
                pltpu.make_async_copy(left_ref.at[last, :, core], left_half, third_sems.at[0]),
                pltpu.make_async_copy(right_ref.at[last], right_third, third_sems.at[1]),
            )

        @pl.when(own >= 0)
        def _():
            for load in third_loads():
                load.start()

    lane = lax.broadcasted_iota(jnp.int32, (1, LANES), 1)
    squares = jnp.zeros((1, LANES), jnp.float32)
    for s in range(slot_count):
        def compute(s=s):
            def left_rows(m):
                left_load(s, m).wait()
                return left[s, m * per_tile : (m + 1) * per_tile].reshape(TILE, block_size)

            def put(m, tile):
                for j in range(lane_tiles):
                    part = tile[:, j * LANES : (j + 1) * LANES].reshape(
                        per_tile, row_halves, SUBLANES, LANES
                    )
                    for h in range(row_halves):
                        out_ref[
                            m * per_tile : (m + 1) * per_tile, (s * row_halves + h) * lane_tiles + j
                        ] = part[:, h]

            return block_product(
                left_rows,
                lambda: recv_ref[:, s * row_count : (s + 1) * row_count, :].reshape(
                    block_size, block_size
                ),
                lambda: right_load(s).wait(),
                lambda: right[s],
                times,
                put,
            )

        value = lax.cond(info_ref[s] >= 0, compute, lambda: jnp.zeros((1, 1), jnp.float32))
        squares = squares + jnp.where(lane == info_ref[s], value, 0.0)
    squares_ref[...] = squares

    if final:
        out_ref[:, out_ref.shape[1] - 1] = jnp.broadcast_to(
            extra_tile(sums_ref[...], squares)[None], (group_size, SUBLANES, LANES)
        )
    else:
        @pl.when(own >= 0)
        def _():
            for load in third_loads():
                load.wait()


def multiply(info, sums, received, left_set, rights, slot_count, total_tiles, final):
    capacity, group_size, row_halves, _, block_size = left_set.shape
    return pl.pallas_call(
        functools.partial(multiply_kernel, slot_count, final),
        out_shape=(
            pltpu.VMEM((group_size, total_tiles, SUBLANES, LANES), jnp.bfloat16),
            jax.ShapeDtypeStruct((1, LANES), jnp.float32),
            pltpu.VMEM((group_size, SUBLANES, block_size), jnp.bfloat16),
            pltpu.VMEM((block_size, block_size), jnp.bfloat16),
        ),
        in_specs=[IN_SMEM, IN_VMEM, IN_VMEM, IN_ANY, IN_ANY],
        out_specs=(IN_VMEM,) * 4,
        scratch_shapes=[
            pltpu.VMEM((slot_count, group_size, row_halves, SUBLANES, block_size), jnp.bfloat16),
            pltpu.VMEM((slot_count, block_size, block_size), jnp.bfloat16),
            pltpu.VMEM((block_size, block_size), jnp.bfloat16),
            pltpu.SemaphoreType.DMA((slot_count, block_size // TILE)),
            pltpu.SemaphoreType.DMA((slot_count,)),
            pltpu.SemaphoreType.DMA((2,)),
        ],
        compiler_params=pltpu.CompilerParams(vmem_limit_bytes=(36 if final else 26) * 2**20),
        cost_estimate=pl.CostEstimate(
            flops=slot_count * 4 * block_size**3,
            bytes_accessed=slot_count * 8 * block_size**2,
            transcendentals=0,
        ),
    )(info, sums, *keep_vmem(received), *keep_hbm(left_set, rights))


def shared_kernel(
    info_ref, sums_ref, squares_ref, own_ref, other_ref, left_ref, right_ref, left_away, right_away,
    before_ref, out_ref,
    grad, times, product, extra, grad_sems, out_sems, extra_sem,
):
    group_size, _, half, block_size = grad.shape
    tile_count = times.shape[0] // TILE
    per_tile = TILE // half
    lane_tiles = product.shape[1]
    first_tile = out_ref.shape[1] - 1 - lane_tiles
    capacity = info_ref.shape[0] - 2
    block = jnp.maximum(info_ref[capacity - 1], info_ref[capacity])
    core = info_ref[capacity + 1]
    del before_ref
    loads = [
        pltpu.make_async_copy(own_ref, grad.at[:, core], grad_sems.at[0]),
        pltpu.make_async_copy(other_ref, grad.at[:, 1 - core], grad_sems.at[1]),
    ]

    def store(m):
        return pltpu.make_async_copy(
            product.at[pl.ds(m * per_tile, per_tile)],
            out_ref.at[pl.ds(m * per_tile, per_tile), pl.ds(first_tile, lane_tiles)],
            out_sems.at[m],
        )

    def compute(left_from, right_from):
        for load in loads:
            load.start()
        for load in loads:
            load.wait()

        def put(m, tile):
            for j in range(lane_tiles):
                product[m * per_tile : (m + 1) * per_tile, j] = tile[
                    :, j * LANES : (j + 1) * LANES
                ].reshape(per_tile, SUBLANES, LANES)
            store(m).start()

        return block_product(
            lambda m: left_from[m * per_tile : (m + 1) * per_tile].reshape(TILE, block_size),
            lambda: grad[...].reshape(block_size, block_size),
            lambda: None,
            lambda: right_from[...],
            times,
            put,
        )

    value = lax.cond(
        info_ref[capacity - 1] >= 0,
        lambda: compute(left_ref, right_ref),
        lambda: lax.cond(
            block >= 0,
            lambda: compute(left_away, right_away),
            lambda: jnp.zeros((1, 1), jnp.float32),
        ),
    )
    lane = lax.broadcasted_iota(jnp.int32, (1, LANES), 1)
    squares = squares_ref[...] + jnp.where(lane == block, value, 0.0)
    extra[...] = jnp.broadcast_to(extra_tile(sums_ref[...], squares)[None, None], extra.shape)
    send_extra = pltpu.make_async_copy(
        extra, out_ref.at[:, pl.ds(out_ref.shape[1] - 1, 1)], extra_sem
    )
    send_extra.start()

    @pl.when(block >= 0)
    def _():
        for m in range(tile_count):
            store(m).wait()

    send_extra.wait()


def multiply_shared(
    info, sums, squares, own, other, left_half, right, left_away, right_away, outgoing
):
    group_size, half, block_size = own.shape
    lane_tiles = block_size // LANES
    rows = group_size * half
    return pl.pallas_call(
        shared_kernel,
        out_shape=pltpu.VMEM(outgoing.shape, outgoing.dtype),
        in_specs=[IN_SMEM, IN_VMEM, IN_VMEM, IN_ANY, IN_ANY] + [IN_VMEM] * 4 + [IN_ANY],
        out_specs=IN_ANY,
        input_output_aliases={9: 0},
        scratch_shapes=[
            pltpu.VMEM((group_size, 2, half, block_size), jnp.bfloat16),
            pltpu.VMEM((rows, block_size), jnp.bfloat16),
            pltpu.VMEM((group_size, lane_tiles, SUBLANES, LANES), jnp.bfloat16),
            pltpu.VMEM((group_size, 1, SUBLANES, LANES), jnp.bfloat16),
            pltpu.SemaphoreType.DMA((2,)),
            pltpu.SemaphoreType.DMA((rows // TILE,)),
            pltpu.SemaphoreType.DMA,
        ],
        compiler_params=pltpu.CompilerParams(vmem_limit_bytes=32 * 2**20),
        cost_estimate=pl.CostEstimate(
            flops=4 * rows * block_size**2, bytes_accessed=8 * rows * block_size, transcendentals=0
        ),
    )(
        info, sums, squares,
        *keep_vmem(own, other, left_half, right, left_away, right_away, outgoing),
    )


def unpack_kernel(full_slots, owner_ref, slot_ref, back_ref, out_ref, stage, out_sems):
    block_rows, row_count, width = stage.shape
    block_count = owner_ref.shape[0]
    block_cols = block_count // block_rows
    block_size = width // block_cols
    row_halves = row_count // SUBLANES
    lane_tiles = block_size // LANES
    last = back_ref.shape[1] - 1
    found = jnp.sum(back_ref[:, last].astype(jnp.float32), axis=0)
    count = float(block_size * block_size)
    rms_adam = jnp.sqrt((found[0:1] + found[1:2] + found[2:3]) / count + eps_norm)
    rms_shampoo = jnp.sqrt((found[3:4] + found[4:5] + found[5:6]) / count + eps_norm)
    scale = rms_adam / rms_shampoo
    writes = []
    for r in range(block_rows):
        for c in range(block_cols):
            b = r * block_cols + c
            factor = jnp.broadcast_to(scale[:, b : b + 1], (SUBLANES, LANES))
            owner, slot = owner_ref[b], slot_ref[b]
            for h in range(row_halves):
                whole = slot < full_slots
                source = jnp.where(whole, owner, 2 * lax.div(owner, 2) + h)
                first = jnp.where(
                    whole, (slot * row_halves + h) * lane_tiles, full_slots * row_halves * lane_tiles
                )
                for j in range(lane_tiles):
                    stage[
                        r,
                        h * SUBLANES : (h + 1) * SUBLANES,
                        c * block_size + j * LANES : c * block_size + (j + 1) * LANES,
                    ] = (back_ref[source, first + j].astype(jnp.float32) * factor).astype(jnp.bfloat16)
        write = pltpu.make_async_copy(stage.at[r], out_ref.at[r], out_sems.at[r])
        write.start()
        writes.append(write)
    for write in writes:
        write.wait()


def unpack(owners, slots, back, shape, full_slots):
    block_rows, row_count, width = shape
    return pl.pallas_call(
        functools.partial(unpack_kernel, full_slots),
        out_shape=pltpu.HBM(shape, jnp.bfloat16),
        in_specs=[IN_SMEM, IN_SMEM, IN_VMEM],
        out_specs=IN_ANY,
        scratch_shapes=[
            pltpu.VMEM(shape, jnp.bfloat16),
            pltpu.SemaphoreType.DMA((block_rows,)),
        ],
        compiler_params=pltpu.CompilerParams(vmem_limit_bytes=32 * 2**20),
        cost_estimate=pl.CostEstimate(
            flops=block_rows * row_count * width,
            bytes_accessed=4 * block_rows * row_count * width,
            transcendentals=0,
        ),
    )(owners, slots, *keep_vmem(back))


def exchange(value):
    return lax.all_to_all(value, "dp", split_axis=0, concat_axis=0, tiled=True)


def on_device(gradient, second_moment, owner_table, left_roots, right_roots):
    group_size = lax.axis_size("dp")
    my_index = lax.axis_index("dp")
    _, row_count, width = gradient.shape
    block_size = left_roots.shape[-1]
    capacity = left_roots.shape[2]
    full = capacity - 1
    half = row_count // 2
    lane_tiles = block_size // LANES
    slot_tiles = lane_tiles * (row_count // SUBLANES)
    owners = owner_table[:, 0]
    me = my_index.reshape(1)
    left_set = left_roots.reshape(capacity, group_size, 2, half, block_size)
    rights = right_roots[0, 0]
    send, sums, slots, info, conflict, left_away, right_away = pack(
        me, owners, gradient, second_moment, left_set, rights, full * row_count + half, full
    )

    def general(send, sums, slots, info, left_away, right_away, gradient, left_set, rights):
        send = pack(
            me, owners, gradient, None, left_set, rights, capacity * row_count, capacity
        )[0]
        outgoing = multiply(
            info, sums, exchange(send), left_set, rights, capacity, capacity * slot_tiles + 1, True,
        )[0]
        return unpack(owners, slots, exchange(outgoing), gradient.shape, capacity)

    def shared(send, sums, slots, info, left_away, right_away, gradient, left_set, rights):
        partner = [(i, i ^ 1) for i in range(group_size)]
        received, left_away, right_away = lax.optimization_barrier(
            (exchange(send), left_away, right_away)
        )
        own = received[:, full * row_count :, :]
        other = lax.ppermute(own, "dp", partner)
        left_away = lax.ppermute(left_away, "dp", partner)
        right_away = lax.ppermute(right_away, "dp", partner)
        outgoing, squares, left_half, right_third = multiply(
            info, sums, received, left_set, rights, full, full * slot_tiles + lane_tiles + 1, False,
        )
        outgoing = multiply_shared(
            info, sums, squares, own, other, left_half, right_third, left_away, right_away, outgoing
        )
        return unpack(owners, slots, exchange(outgoing), gradient.shape, full)

    return lax.cond(
        conflict[0] > 0, general, shared,
        send, sums, slots, info, left_away, right_away, gradient, left_set, rights,
    )


def solution(mesh):
    return jax.shard_map(
        on_device,
        mesh=mesh,
        in_specs=(
            P(None, "dp", "mp"),
            P(None, "dp", "mp"),
            P(),
            P("dp", "mp", None, None, None),
            P("dp", "mp", None, None, None),
        ),
        out_specs=P(None, "dp", "mp"),
        check_vma=False,
    )
```

```python
import functools

import jax
import jax.numpy as jnp
from jax import lax
from jax.experimental import pallas as pl
from jax.experimental.pallas import tpu as pltpu
from jax.sharding import PartitionSpec as P

beta_two = 0.95
eps_adam = 1e-08
eps_norm = 1e-06

TILE = 256
LANES = 128
SUBLANES = 16
IN_VMEM = pl.BlockSpec(memory_space=pltpu.VMEM)
IN_SMEM = pl.BlockSpec(memory_space=pltpu.SMEM)
IN_ANY = pl.BlockSpec(memory_space=pl.ANY)


def keep_hbm(*values):
    return [pltpu.with_memory_space_constraint(value, pltpu.HBM) for value in values]


def keep_vmem(*values):
    return [pltpu.with_memory_space_constraint(value, pltpu.VMEM) for value in values]


def pack_kernel(
    full_slots, capacity, first_pass, me_ref, owner_ref, grad_ref, moment_ref, left_ref, right_ref,
    send_ref, sums_ref, slot_ref, info_ref, conflict_ref, left_away, right_away,
    counts, table, stage, moments, partial, stage_sems, away_sems,
):
    block_rows, row_count, width = grad_ref.shape
    group_size, _, block_size = send_ref.shape
    block_cols = width // block_size
    half = row_count // 2
    pairs = [(grad_ref, stage)] + ([(moment_ref, moments)] if first_pass else [])
    loads = [
        [
            pltpu.make_async_copy(source.at[r], target.at[r], stage_sems.at[i, r])
            for i, (source, target) in enumerate(pairs)
        ]
        for r in range(block_rows)
    ]
    for row in loads:
        for load in row:
            load.start()
    me = me_ref[0]
    core = lax.rem(me, 2)
    if first_pass:
        away = [
            pltpu.make_async_copy(left_ref.at[capacity - 1, :, 1 - core], left_away, away_sems.at[0]),
            pltpu.make_async_copy(right_ref.at[capacity - 1], right_away, away_sems.at[1]),
        ]
        for copy in away:
            copy.start()

    for index in range(group_size):
        counts[index] = 0
        for slot in range(capacity):
            table[index * capacity + slot] = -1
    conflict_ref[0] = 0
    partial[...] = jnp.zeros(partial.shape, jnp.float32)

    def block(r, c):
        b = r * block_cols + c
        owner = owner_ref[b]
        slot = counts[owner]
        counts[owner] = slot + 1
        slot_ref[b] = slot
        columns = pl.ds(pl.multiple_of(c * block_size, block_size), block_size)
        shared = slot >= full_slots
        for h in range(2):
            target = jnp.where(shared, owner - lax.rem(owner, 2) + h, owner)
            start = jnp.where(shared, full_slots * row_count, slot * row_count + h * half)
            send_ref[target, pl.ds(pl.multiple_of(start, half), half), :] = stage[
                r, h * half : (h + 1) * half, columns
            ]
        partner = owner + 1 - 2 * lax.rem(owner, 2)
        taken = table[partner * capacity + capacity - 1] >= 0
        conflict_ref[0] = conflict_ref[0] | (shared & taken).astype(jnp.int32)
        table[owner * capacity + slot] = b
        if first_pass:
            total = jnp.zeros((8, LANES), jnp.float32)
            for k in range(0, block_size, 2 * LANES):
                part = pl.ds(pl.multiple_of(c * block_size + k, 2 * LANES), 2 * LANES)
                wide = stage[r, :, part].astype(jnp.float32)
                moment = beta_two * moments[r, :, part].astype(jnp.float32) + (
                    (1.0 - beta_two) * wide * wide
                )
                direction = wide / (jnp.sqrt(moment) + eps_adam)
                value = jnp.sum((direction * direction).reshape(row_count // 8, 8, -1), axis=0)
                total = total + value[:, :LANES] + value[:, LANES:]
            partial[pl.ds(b, 1), :] = jnp.sum(total, axis=0, keepdims=True)

    for r in range(block_rows):
        for load in loads[r]:
            load.wait()
        for c in range(block_cols):
            block(r, c)

    for slot in range(capacity):
        info_ref[slot] = table[me * capacity + slot]
    info_ref[capacity] = table[(me + 1 - 2 * core) * capacity + capacity - 1]
    info_ref[capacity + 1] = core
    sums_ref[...] = lax.dot_general(
        jnp.ones((8, LANES), jnp.float32),
        partial[...],
        (((1,), (1,)), ((), ())),
        precision=lax.Precision.HIGHEST,
        preferred_element_type=jnp.float32,
    )[0:1]
    if first_pass:
        for copy in away:
            copy.wait()


def pack(me, owners, gradient, second_moment, left_set, rights, rows, full_slots):
    first_pass = second_moment is not None
    capacity, group_size, _, half, block_size = left_set.shape
    return pl.pallas_call(
        functools.partial(pack_kernel, full_slots, capacity, first_pass),
        out_shape=(
            pltpu.VMEM((group_size, rows, block_size), jnp.bfloat16),
            jax.ShapeDtypeStruct((1, LANES), jnp.float32),
            jax.ShapeDtypeStruct(owners.shape, jnp.int32),
            jax.ShapeDtypeStruct((capacity + 2,), jnp.int32),
            jax.ShapeDtypeStruct((1,), jnp.int32),
            pltpu.VMEM((group_size, half, block_size), jnp.bfloat16),
            pltpu.VMEM((block_size, block_size), jnp.bfloat16),
        ),
        in_specs=[IN_SMEM, IN_SMEM] + [IN_ANY] * 4,
        out_specs=(IN_VMEM, IN_VMEM, IN_SMEM, IN_SMEM, IN_SMEM, IN_VMEM, IN_VMEM),
        scratch_shapes=[
            pltpu.SMEM((group_size,), jnp.int32),
            pltpu.SMEM((group_size * capacity,), jnp.int32),
            pltpu.VMEM(gradient.shape, jnp.bfloat16),
            pltpu.VMEM(gradient.shape, jnp.bfloat16),
            pltpu.VMEM((LANES, LANES), jnp.float32),
            pltpu.SemaphoreType.DMA((2, gradient.shape[0])),
            pltpu.SemaphoreType.DMA((2,)),
        ],
        compiler_params=pltpu.CompilerParams(vmem_limit_bytes=24 * 2**20),
        cost_estimate=pl.CostEstimate(
            flops=10 * gradient.size, bytes_accessed=8 * gradient.size, transcendentals=2 * gradient.size
        ),
    )(
        me,
        owners,
        *keep_hbm(gradient, second_moment if first_pass else gradient, left_set, rights),
    )


def three_parts(value):
    high = value.astype(jnp.bfloat16)
    rest = value - high.astype(jnp.float32)
    middle = rest.astype(jnp.bfloat16)
    low = (rest - middle.astype(jnp.float32)).astype(jnp.bfloat16)
    return high, middle, low


def extra_tile(sums, squares):
    rows = lax.broadcasted_iota(jnp.int32, (SUBLANES, LANES), 0)
    content = jnp.zeros((SUBLANES, LANES), jnp.float32)
    for i, part in enumerate([*three_parts(sums), *three_parts(squares)]):
        content = jnp.where(rows == i, part.astype(jnp.float32), content)
    return content.astype(jnp.bfloat16)


def block_product(left_rows, grad, right, times, put):
    count = times.shape[0] // TILE
    for m in range(count):
        times[m * TILE : (m + 1) * TILE, :] = jnp.dot(
            left_rows(m), grad(), preferred_element_type=jnp.float32
        ).astype(jnp.bfloat16)
    total = jnp.zeros((8, times.shape[1]), jnp.float32)
    for m in range(count):
        value = jnp.dot(
            times[m * TILE : (m + 1) * TILE, :], right(), preferred_element_type=jnp.float32
        )
        total = total + jnp.sum((value * value).reshape(TILE // 8, 8, -1), axis=0)
        put(m, value.astype(jnp.bfloat16))
    return jnp.sum(jnp.sum(total, axis=0, keepdims=True), axis=1, keepdims=True)


def multiply_kernel(
    slot_count, final, info_ref, sums_ref, recv_ref, left_ref, right_ref, out_ref, squares_ref, times
):
    _, group_size, row_halves, _, block_size = left_ref.shape
    row_count = row_halves * SUBLANES
    per_tile = TILE // row_count
    lane_tiles = block_size // LANES
    lane = lax.broadcasted_iota(jnp.int32, (1, LANES), 1)
    squares = jnp.zeros((1, LANES), jnp.float32)
    for s in range(slot_count):
        def compute(s=s):
            def put(m, tile):
                for j in range(lane_tiles):
                    part = tile[:, j * LANES : (j + 1) * LANES].reshape(
                        per_tile, row_halves, SUBLANES, LANES
                    )
                    for h in range(row_halves):
                        out_ref[
                            m * per_tile : (m + 1) * per_tile, (s * row_halves + h) * lane_tiles + j
                        ] = part[:, h]

            return block_product(
                lambda m: left_ref[s, m * per_tile : (m + 1) * per_tile].reshape(TILE, block_size),
                lambda: recv_ref[:, s * row_count : (s + 1) * row_count, :].reshape(
                    block_size, block_size
                ),
                lambda: right_ref[s],
                times,
                put,
            )

        value = lax.cond(info_ref[s] >= 0, compute, lambda: jnp.zeros((1, 1), jnp.float32))
        squares = squares + jnp.where(lane == info_ref[s], value, 0.0)
    squares_ref[...] = squares
    if final:
        out_ref[:, out_ref.shape[1] - 1] = jnp.broadcast_to(
            extra_tile(sums_ref[...], squares)[None], (group_size, SUBLANES, LANES)
        )


def multiply(info, sums, received, left_set, rights, slot_count, total_tiles, final):
    _, group_size, _, _, block_size = left_set.shape
    return pl.pallas_call(
        functools.partial(multiply_kernel, slot_count, final),
        out_shape=(
            pltpu.VMEM((group_size, total_tiles, SUBLANES, LANES), jnp.bfloat16),
            jax.ShapeDtypeStruct((1, LANES), jnp.float32),
        ),
        in_specs=[IN_SMEM] + [IN_VMEM] * 4,
        out_specs=(IN_VMEM, IN_VMEM),
        scratch_shapes=[pltpu.VMEM((block_size, block_size), jnp.bfloat16)],
        compiler_params=pltpu.CompilerParams(vmem_limit_bytes=12 * 2**20),
        cost_estimate=pl.CostEstimate(
            flops=slot_count * 4 * block_size**3,
            bytes_accessed=slot_count * 8 * block_size**2,
            transcendentals=0,
        ),
    )(info, sums, *keep_vmem(received, left_set, rights))


def shared_kernel(
    info_ref, sums_ref, squares_ref, own_ref, other_ref, left_ref, right_ref, left_away, right_away,
    before_ref, out_ref,
    grad, times, product, extra, grad_sems, out_sems, extra_sem,
):
    group_size, _, half, block_size = grad.shape
    tile_count = times.shape[0] // TILE
    per_tile = TILE // half
    lane_tiles = product.shape[1]
    first_tile = out_ref.shape[1] - 1 - lane_tiles
    capacity = info_ref.shape[0] - 2
    block = jnp.maximum(info_ref[capacity - 1], info_ref[capacity])
    core = info_ref[capacity + 1]
    del before_ref
    loads = [
        pltpu.make_async_copy(own_ref, grad.at[:, core], grad_sems.at[0]),
        pltpu.make_async_copy(other_ref, grad.at[:, 1 - core], grad_sems.at[1]),
    ]

    def store(m):
        return pltpu.make_async_copy(
            product.at[pl.ds(m * per_tile, per_tile)],
            out_ref.at[pl.ds(m * per_tile, per_tile), pl.ds(first_tile, lane_tiles)],
            out_sems.at[m],
        )

    def compute(left_from, right_from):
        for load in loads:
            load.start()
        for load in loads:
            load.wait()

        def put(m, tile):
            for j in range(lane_tiles):
                product[m * per_tile : (m + 1) * per_tile, j] = tile[
                    :, j * LANES : (j + 1) * LANES
                ].reshape(per_tile, SUBLANES, LANES)
            store(m).start()

        return block_product(
            lambda m: left_from[m * per_tile : (m + 1) * per_tile].reshape(TILE, block_size),
            lambda: grad[...].reshape(block_size, block_size),
            lambda: right_from[...],
            times,
            put,
        )

    value = lax.cond(
        info_ref[capacity - 1] >= 0,
        lambda: compute(left_ref.at[capacity - 1, :, core], right_ref.at[capacity - 1]),
        lambda: lax.cond(
            block >= 0,
            lambda: compute(left_away, right_away),
            lambda: jnp.zeros((1, 1), jnp.float32),
        ),
    )
    lane = lax.broadcasted_iota(jnp.int32, (1, LANES), 1)
    squares = squares_ref[...] + jnp.where(lane == block, value, 0.0)
    extra[...] = jnp.broadcast_to(extra_tile(sums_ref[...], squares)[None, None], extra.shape)
    send_extra = pltpu.make_async_copy(
        extra, out_ref.at[:, pl.ds(out_ref.shape[1] - 1, 1)], extra_sem
    )
    send_extra.start()

    @pl.when(block >= 0)
    def _():
        for m in range(tile_count):
            store(m).wait()

    send_extra.wait()


def multiply_shared(
    info, sums, squares, own, other, left_set, rights, left_away, right_away, outgoing
):
    group_size, half, block_size = own.shape
    lane_tiles = block_size // LANES
    rows = group_size * half
    return pl.pallas_call(
        shared_kernel,
        out_shape=pltpu.VMEM(outgoing.shape, outgoing.dtype),
        in_specs=[IN_SMEM, IN_VMEM, IN_VMEM, IN_ANY, IN_ANY] + [IN_VMEM] * 4 + [IN_ANY],
        out_specs=IN_ANY,
        input_output_aliases={9: 0},
        scratch_shapes=[
            pltpu.VMEM((group_size, 2, half, block_size), jnp.bfloat16),
            pltpu.VMEM((rows, block_size), jnp.bfloat16),
            pltpu.VMEM((group_size, lane_tiles, SUBLANES, LANES), jnp.bfloat16),
            pltpu.VMEM((group_size, 1, SUBLANES, LANES), jnp.bfloat16),
            pltpu.SemaphoreType.DMA((2,)),
            pltpu.SemaphoreType.DMA((rows // TILE,)),
            pltpu.SemaphoreType.DMA,
        ],
        compiler_params=pltpu.CompilerParams(vmem_limit_bytes=14 * 2**20),
        cost_estimate=pl.CostEstimate(
            flops=4 * rows * block_size**2, bytes_accessed=8 * rows * block_size, transcendentals=0
        ),
    )(
        info, sums, squares,
        *keep_vmem(own, other, left_set, rights, left_away, right_away, outgoing),
    )


def unpack_kernel(full_slots, owner_ref, slot_ref, back_ref, out_ref, stage, out_sems):
    block_rows, row_count, width = stage.shape
    block_count = owner_ref.shape[0]
    block_cols = block_count // block_rows
    block_size = width // block_cols
    row_halves = row_count // SUBLANES
    lane_tiles = block_size // LANES
    last = back_ref.shape[1] - 1
    found = jnp.sum(back_ref[:, last].astype(jnp.float32), axis=0)
    count = float(block_size * block_size)
    rms_adam = jnp.sqrt((found[0:1] + found[1:2] + found[2:3]) / count + eps_norm)
    rms_shampoo = jnp.sqrt((found[3:4] + found[4:5] + found[5:6]) / count + eps_norm)
    scale = rms_adam / rms_shampoo
    writes = []
    for r in range(block_rows):
        for c in range(block_cols):
            b = r * block_cols + c
            factor = jnp.broadcast_to(scale[:, b : b + 1], (SUBLANES, LANES))
            owner, slot = owner_ref[b], slot_ref[b]
            for h in range(row_halves):
                whole = slot < full_slots
                source = jnp.where(whole, owner, 2 * lax.div(owner, 2) + h)
                first = jnp.where(
                    whole, (slot * row_halves + h) * lane_tiles, full_slots * row_halves * lane_tiles
                )
                for j in range(lane_tiles):
                    stage[
                        r,
                        h * SUBLANES : (h + 1) * SUBLANES,
                        c * block_size + j * LANES : c * block_size + (j + 1) * LANES,
                    ] = (back_ref[source, first + j].astype(jnp.float32) * factor).astype(jnp.bfloat16)
        write = pltpu.make_async_copy(stage.at[r], out_ref.at[r], out_sems.at[r])
        write.start()
        writes.append(write)
    for write in writes:
        write.wait()


def unpack(owners, slots, back, shape, full_slots):
    block_rows, row_count, width = shape
    return pl.pallas_call(
        functools.partial(unpack_kernel, full_slots),
        out_shape=pltpu.HBM(shape, jnp.bfloat16),
        in_specs=[IN_SMEM, IN_SMEM, IN_VMEM],
        out_specs=IN_ANY,
        scratch_shapes=[
            pltpu.VMEM(shape, jnp.bfloat16),
            pltpu.SemaphoreType.DMA((block_rows,)),
        ],
        compiler_params=pltpu.CompilerParams(vmem_limit_bytes=32 * 2**20),
        cost_estimate=pl.CostEstimate(
            flops=block_rows * row_count * width,
            bytes_accessed=4 * block_rows * row_count * width,
            transcendentals=0,
        ),
    )(owners, slots, *keep_vmem(back))


def exchange(value):
    return lax.all_to_all(value, "dp", split_axis=0, concat_axis=0, tiled=True)


def on_device(gradient, second_moment, owner_table, left_roots, right_roots):
    group_size = lax.axis_size("dp")
    my_index = lax.axis_index("dp")
    _, row_count, width = gradient.shape
    block_size = left_roots.shape[-1]
    capacity = left_roots.shape[2]
    full = capacity - 1
    half = row_count // 2
    lane_tiles = block_size // LANES
    slot_tiles = lane_tiles * (row_count // SUBLANES)
    owners = owner_table[:, 0]
    me = my_index.reshape(1)
    left_set = left_roots.reshape(capacity, group_size, 2, half, block_size)
    rights = right_roots[0, 0]
    send, sums, slots, info, conflict, left_away, right_away = pack(
        me, owners, gradient, second_moment, left_set, rights, full * row_count + half, full
    )

    def general(send, sums, slots, info, left_away, right_away, gradient, left_set, rights):
        send = pack(
            me, owners, gradient, None, left_set, rights, capacity * row_count, capacity
        )[0]
        outgoing = multiply(
            info, sums, exchange(send), left_set, rights, capacity, capacity * slot_tiles + 1, True,
        )[0]
        return unpack(owners, slots, exchange(outgoing), gradient.shape, capacity)

    def shared(send, sums, slots, info, left_away, right_away, gradient, left_set, rights):
        partner = [(i, i ^ 1) for i in range(group_size)]
        received, left_away, right_away = lax.optimization_barrier(
            (exchange(send), left_away, right_away)
        )
        own = received[:, full * row_count :, :]
        other = lax.ppermute(own, "dp", partner)
        left_away = lax.ppermute(left_away, "dp", partner)
        right_away = lax.ppermute(right_away, "dp", partner)
        outgoing, squares = multiply(
            info, sums, received, left_set, rights, full, full * slot_tiles + lane_tiles + 1, False,
        )
        outgoing = multiply_shared(
            info, sums, squares, own, other, left_set, rights, left_away, right_away, outgoing
        )
        return unpack(owners, slots, exchange(outgoing), gradient.shape, full)

    return lax.cond(
        conflict[0] > 0, general, shared,
        send, sums, slots, info, left_away, right_away, gradient, left_set, rights,
    )


def solution(mesh):
    return jax.shard_map(
        on_device,
        mesh=mesh,
        in_specs=(
            P(None, "dp", "mp"),
            P(None, "dp", "mp"),
            P(),
            P("dp", "mp", None, None, None),
            P("dp", "mp", None, None, None),
        ),
        out_specs=P(None, "dp", "mp"),
        check_vma=False,
    )
```

```python
import functools

import jax
import jax.numpy as jnp
from jax import lax
from jax.experimental import pallas as pl
from jax.experimental.pallas import tpu as pltpu
from jax.sharding import PartitionSpec as P

beta_two = 0.95
eps_adam = 1e-08
eps_norm = 1e-06

TILE = 256
LANES = 128
SUBLANES = 16
IN_VMEM = pl.BlockSpec(memory_space=pltpu.VMEM)
IN_SMEM = pl.BlockSpec(memory_space=pltpu.SMEM)
IN_ANY = pl.BlockSpec(memory_space=pl.ANY)


def keep_hbm(*values):
    return [pltpu.with_memory_space_constraint(value, pltpu.HBM) for value in values]


def keep_vmem(*values):
    return [pltpu.with_memory_space_constraint(value, pltpu.VMEM) for value in values]


def pack_kernel(
    full_slots, capacity, first_pass, me_ref, owner_ref, grad_ref, moment_ref, left_ref, right_ref,
    send_ref, sums_ref, slot_ref, info_ref, conflict_ref, left_away, right_away,
    counts, table, stage, moments, partial, stage_sems, away_sems,
):
    block_rows, row_count, width = grad_ref.shape
    group_size, _, block_size = send_ref.shape
    block_cols = width // block_size
    half = row_count // 2
    pairs = [(grad_ref, stage)] + ([(moment_ref, moments)] if first_pass else [])
    loads = [
        [
            pltpu.make_async_copy(source.at[r], target.at[r], stage_sems.at[i, r])
            for i, (source, target) in enumerate(pairs)
        ]
        for r in range(block_rows)
    ]
    for row in loads:
        for load in row:
            load.start()
    me = me_ref[0]
    core = lax.rem(me, 2)
    if first_pass:
        away = [
            pltpu.make_async_copy(left_ref.at[capacity - 1, :, 1 - core], left_away, away_sems.at[0]),
            pltpu.make_async_copy(right_ref.at[capacity - 1], right_away, away_sems.at[1]),
        ]
        for copy in away:
            copy.start()

    for index in range(group_size):
        counts[index] = 0
        for slot in range(capacity):
            table[index * capacity + slot] = -1
    conflict_ref[0] = 0
    partial[...] = jnp.zeros(partial.shape, jnp.float32)

    def block(r, c):
        b = r * block_cols + c
        owner = owner_ref[b]
        slot = counts[owner]
        counts[owner] = slot + 1
        slot_ref[b] = slot
        columns = pl.ds(pl.multiple_of(c * block_size, block_size), block_size)
        shared = slot >= full_slots
        for h in range(2):
            target = jnp.where(shared, owner - lax.rem(owner, 2) + h, owner)
            start = jnp.where(shared, full_slots * row_count, slot * row_count + h * half)
            send_ref[target, pl.ds(pl.multiple_of(start, half), half), :] = stage[
                r, h * half : (h + 1) * half, columns
            ]
        partner = owner + 1 - 2 * lax.rem(owner, 2)
        taken = table[partner * capacity + capacity - 1] >= 0
        conflict_ref[0] = conflict_ref[0] | (shared & taken).astype(jnp.int32)
        table[owner * capacity + slot] = b
        if first_pass:
            total = jnp.zeros((8, LANES), jnp.float32)
            for k in range(0, block_size, 2 * LANES):
                part = pl.ds(pl.multiple_of(c * block_size + k, 2 * LANES), 2 * LANES)
                wide = stage[r, :, part].astype(jnp.float32)
                moment = beta_two * moments[r, :, part].astype(jnp.float32) + (
                    (1.0 - beta_two) * wide * wide
                )
                direction = wide / (jnp.sqrt(moment) + eps_adam)
                value = jnp.sum((direction * direction).reshape(row_count // 8, 8, -1), axis=0)
                total = total + value[:, :LANES] + value[:, LANES:]
            partial[pl.ds(b, 1), :] = jnp.sum(total, axis=0, keepdims=True)

    for r in range(block_rows):
        for load in loads[r]:
            load.wait()
        for c in range(block_cols):
            block(r, c)

    for slot in range(capacity):
        info_ref[slot] = table[me * capacity + slot]
    info_ref[capacity] = table[(me + 1 - 2 * core) * capacity + capacity - 1]
    info_ref[capacity + 1] = core
    sums_ref[...] = lax.dot_general(
        jnp.ones((8, LANES), jnp.float32),
        partial[...],
        (((1,), (1,)), ((), ())),
        precision=lax.Precision.HIGHEST,
        preferred_element_type=jnp.float32,
    )[0:1]
    if first_pass:
        for copy in away:
            copy.wait()


def pack(me, owners, gradient, second_moment, left_set, rights, rows, full_slots):
    first_pass = second_moment is not None
    capacity, group_size, _, half, block_size = left_set.shape
    return pl.pallas_call(
        functools.partial(pack_kernel, full_slots, capacity, first_pass),
        out_shape=(
            pltpu.VMEM((group_size, rows, block_size), jnp.bfloat16),
            jax.ShapeDtypeStruct((1, LANES), jnp.float32),
            jax.ShapeDtypeStruct(owners.shape, jnp.int32),
            jax.ShapeDtypeStruct((capacity + 2,), jnp.int32),
            jax.ShapeDtypeStruct((1,), jnp.int32),
            pltpu.VMEM((group_size, half, block_size), jnp.bfloat16),
            pltpu.VMEM((block_size, block_size), jnp.bfloat16),
        ),
        in_specs=[IN_SMEM, IN_SMEM] + [IN_ANY] * 4,
        out_specs=(IN_VMEM, IN_VMEM, IN_SMEM, IN_SMEM, IN_SMEM, IN_VMEM, IN_VMEM),
        scratch_shapes=[
            pltpu.SMEM((group_size,), jnp.int32),
            pltpu.SMEM((group_size * capacity,), jnp.int32),
            pltpu.VMEM(gradient.shape, jnp.bfloat16),
            pltpu.VMEM(gradient.shape, jnp.bfloat16),
            pltpu.VMEM((LANES, LANES), jnp.float32),
            pltpu.SemaphoreType.DMA((2, gradient.shape[0])),
            pltpu.SemaphoreType.DMA((2,)),
        ],
        compiler_params=pltpu.CompilerParams(vmem_limit_bytes=24 * 2**20),
        cost_estimate=pl.CostEstimate(
            flops=10 * gradient.size, bytes_accessed=8 * gradient.size, transcendentals=2 * gradient.size
        ),
    )(
        me,
        owners,
        *keep_hbm(gradient, second_moment if first_pass else gradient, left_set, rights),
    )


def three_parts(value):
    high = value.astype(jnp.bfloat16)
    rest = value - high.astype(jnp.float32)
    middle = rest.astype(jnp.bfloat16)
    low = (rest - middle.astype(jnp.float32)).astype(jnp.bfloat16)
    return high, middle, low


def extra_tile(sums, squares):
    rows = lax.broadcasted_iota(jnp.int32, (SUBLANES, LANES), 0)
    content = jnp.zeros((SUBLANES, LANES), jnp.float32)
    for i, part in enumerate([*three_parts(sums), *three_parts(squares)]):
        content = jnp.where(rows == i, part.astype(jnp.float32), content)
    return content.astype(jnp.bfloat16)


def block_product(left_rows, grad, right, times, put):
    count = times.shape[0] // TILE
    for m in range(count):
        times[m * TILE : (m + 1) * TILE, :] = jnp.dot(
            left_rows(m), grad(), preferred_element_type=jnp.float32
        ).astype(jnp.bfloat16)
    total = jnp.zeros((8, times.shape[1]), jnp.float32)
    for m in range(count):
        value = jnp.dot(
            times[m * TILE : (m + 1) * TILE, :], right(), preferred_element_type=jnp.float32
        )
        total = total + jnp.sum((value * value).reshape(TILE // 8, 8, -1), axis=0)
        put(m, value.astype(jnp.bfloat16))
    return jnp.sum(jnp.sum(total, axis=0, keepdims=True), axis=1, keepdims=True)


def multiply_kernel(
    slot_count, final, info_ref, sums_ref, recv_ref, left_ref, right_ref, out_ref, squares_ref, times
):
    _, group_size, row_halves, _, block_size = left_ref.shape
    row_count = row_halves * SUBLANES
    per_tile = TILE // row_count
    lane_tiles = block_size // LANES
    lane = lax.broadcasted_iota(jnp.int32, (1, LANES), 1)
    squares = jnp.zeros((1, LANES), jnp.float32)
    for s in range(slot_count):
        def compute(s=s):
            def put(m, tile):
                for j in range(lane_tiles):
                    part = tile[:, j * LANES : (j + 1) * LANES].reshape(
                        per_tile, row_halves, SUBLANES, LANES
                    )
                    for h in range(row_halves):
                        out_ref[
                            m * per_tile : (m + 1) * per_tile, (s * row_halves + h) * lane_tiles + j
                        ] = part[:, h]

            return block_product(
                lambda m: left_ref[s, m * per_tile : (m + 1) * per_tile].reshape(TILE, block_size),
                lambda: recv_ref[:, s * row_count : (s + 1) * row_count, :].reshape(
                    block_size, block_size
                ),
                lambda: right_ref[s],
                times,
                put,
            )

        value = lax.cond(info_ref[s] >= 0, compute, lambda: jnp.zeros((1, 1), jnp.float32))
        squares = squares + jnp.where(lane == info_ref[s], value, 0.0)
    squares_ref[...] = squares
    if final:
        out_ref[:, out_ref.shape[1] - 1] = jnp.broadcast_to(
            extra_tile(sums_ref[...], squares)[None], (group_size, SUBLANES, LANES)
        )


def multiply(info, sums, received, left_set, rights, slot_count, total_tiles, final):
    _, group_size, _, _, block_size = left_set.shape
    return pl.pallas_call(
        functools.partial(multiply_kernel, slot_count, final),
        out_shape=(
            pltpu.VMEM((group_size, total_tiles, SUBLANES, LANES), jnp.bfloat16),
            jax.ShapeDtypeStruct((1, LANES), jnp.float32),
        ),
        in_specs=[IN_SMEM] + [IN_VMEM] * 4,
        out_specs=(IN_VMEM, IN_VMEM),
        scratch_shapes=[pltpu.VMEM((block_size, block_size), jnp.bfloat16)],
        compiler_params=pltpu.CompilerParams(vmem_limit_bytes=12 * 2**20),
        cost_estimate=pl.CostEstimate(
            flops=slot_count * 4 * block_size**3,
            bytes_accessed=slot_count * 8 * block_size**2,
            transcendentals=0,
        ),
    )(info, sums, *keep_vmem(received, left_set, rights))


def shared_kernel(
    info_ref, sums_ref, squares_ref, own_ref, other_ref, left_ref, right_ref, left_away, right_away,
    before_ref, out_ref, grad, times,
):
    group_size, _, half, block_size = grad.shape
    per_tile = TILE // half
    lane_tiles = block_size // LANES
    first_tile = out_ref.shape[1] - 1 - lane_tiles
    capacity = info_ref.shape[0] - 2
    block = jnp.maximum(info_ref[capacity - 1], info_ref[capacity])
    core = info_ref[capacity + 1]
    del before_ref

    def compute(left_from, right_from):
        grad[:, pl.ds(core, 1)] = own_ref[...][:, None]
        grad[:, pl.ds(1 - core, 1)] = other_ref[...][:, None]

        def put(m, tile):
            for j in range(lane_tiles):
                out_ref[m * per_tile : (m + 1) * per_tile, first_tile + j] = tile[
                    :, j * LANES : (j + 1) * LANES
                ].reshape(per_tile, SUBLANES, LANES)

        return block_product(
            lambda m: left_from[m * per_tile : (m + 1) * per_tile].reshape(TILE, block_size),
            lambda: grad[...].reshape(block_size, block_size),
            lambda: right_from[...],
            times,
            put,
        )

    value = lax.cond(
        info_ref[capacity - 1] >= 0,
        lambda: compute(left_ref.at[capacity - 1, :, core], right_ref.at[capacity - 1]),
        lambda: lax.cond(
            block >= 0,
            lambda: compute(left_away, right_away),
            lambda: jnp.zeros((1, 1), jnp.float32),
        ),
    )
    lane = lax.broadcasted_iota(jnp.int32, (1, LANES), 1)
    squares = squares_ref[...] + jnp.where(lane == block, value, 0.0)
    out_ref[:, out_ref.shape[1] - 1] = jnp.broadcast_to(
        extra_tile(sums_ref[...], squares)[None], (group_size, SUBLANES, LANES)
    )


def multiply_shared(
    info, sums, squares, own, other, left_set, rights, left_away, right_away, outgoing
):
    group_size, half, block_size = own.shape
    rows = group_size * half
    return pl.pallas_call(
        shared_kernel,
        out_shape=pltpu.VMEM(outgoing.shape, outgoing.dtype),
        in_specs=[IN_SMEM] + [IN_VMEM] * 9,
        out_specs=IN_VMEM,
        input_output_aliases={9: 0},
        scratch_shapes=[
            pltpu.VMEM((group_size, 2, half, block_size), jnp.bfloat16),
            pltpu.VMEM((rows, block_size), jnp.bfloat16),
        ],
        compiler_params=pltpu.CompilerParams(vmem_limit_bytes=14 * 2**20),
        cost_estimate=pl.CostEstimate(
            flops=4 * rows * block_size**2, bytes_accessed=8 * rows * block_size, transcendentals=0
        ),
    )(
        info, sums, squares,
        *keep_vmem(own, other, left_set, rights, left_away, right_away, outgoing),
    )


def unpack_kernel(full_slots, owner_ref, slot_ref, back_ref, out_ref, stage, out_sems):
    block_rows, row_count, width = stage.shape
    block_count = owner_ref.shape[0]
    block_cols = block_count // block_rows
    block_size = width // block_cols
    row_halves = row_count // SUBLANES
    lane_tiles = block_size // LANES
    last = back_ref.shape[1] - 1
    found = jnp.sum(back_ref[:, last].astype(jnp.float32), axis=0)
    count = float(block_size * block_size)
    rms_adam = jnp.sqrt((found[0:1] + found[1:2] + found[2:3]) / count + eps_norm)
    rms_shampoo = jnp.sqrt((found[3:4] + found[4:5] + found[5:6]) / count + eps_norm)
    scale = rms_adam / rms_shampoo
    writes = []
    for r in range(block_rows):
        for c in range(block_cols):
            b = r * block_cols + c
            factor = jnp.broadcast_to(scale[:, b : b + 1], (SUBLANES, LANES))
            owner, slot = owner_ref[b], slot_ref[b]
            for h in range(row_halves):
                whole = slot < full_slots
                source = jnp.where(whole, owner, 2 * lax.div(owner, 2) + h)
                first = jnp.where(
                    whole, (slot * row_halves + h) * lane_tiles, full_slots * row_halves * lane_tiles
                )
                for j in range(lane_tiles):
                    stage[
                        r,
                        h * SUBLANES : (h + 1) * SUBLANES,
                        c * block_size + j * LANES : c * block_size + (j + 1) * LANES,
                    ] = (back_ref[source, first + j].astype(jnp.float32) * factor).astype(jnp.bfloat16)
        write = pltpu.make_async_copy(stage.at[r], out_ref.at[r], out_sems.at[r])
        write.start()
        writes.append(write)
    for write in writes:
        write.wait()


def unpack(owners, slots, back, shape, full_slots):
    block_rows, row_count, width = shape
    return pl.pallas_call(
        functools.partial(unpack_kernel, full_slots),
        out_shape=pltpu.HBM(shape, jnp.bfloat16),
        in_specs=[IN_SMEM, IN_SMEM, IN_VMEM],
        out_specs=IN_ANY,
        scratch_shapes=[
            pltpu.VMEM(shape, jnp.bfloat16),
            pltpu.SemaphoreType.DMA((block_rows,)),
        ],
        compiler_params=pltpu.CompilerParams(vmem_limit_bytes=32 * 2**20),
        cost_estimate=pl.CostEstimate(
            flops=block_rows * row_count * width,
            bytes_accessed=4 * block_rows * row_count * width,
            transcendentals=0,
        ),
    )(owners, slots, *keep_vmem(back))


def exchange(value):
    return lax.all_to_all(value, "dp", split_axis=0, concat_axis=0, tiled=True)


def on_device(gradient, second_moment, owner_table, left_roots, right_roots):
    group_size = lax.axis_size("dp")
    my_index = lax.axis_index("dp")
    _, row_count, width = gradient.shape
    block_size = left_roots.shape[-1]
    capacity = left_roots.shape[2]
    full = capacity - 1
    half = row_count // 2
    lane_tiles = block_size // LANES
    slot_tiles = lane_tiles * (row_count // SUBLANES)
    owners = owner_table[:, 0]
    me = my_index.reshape(1)
    left_set = left_roots.reshape(capacity, group_size, 2, half, block_size)
    rights = right_roots[0, 0]
    send, sums, slots, info, conflict, left_away, right_away = pack(
        me, owners, gradient, second_moment, left_set, rights, full * row_count + half, full
    )

    def general(send, sums, slots, info, left_away, right_away, gradient, left_set, rights):
        send = pack(
            me, owners, gradient, None, left_set, rights, capacity * row_count, capacity
        )[0]
        outgoing = multiply(
            info, sums, exchange(send), left_set, rights, capacity, capacity * slot_tiles + 1, True,
        )[0]
        return unpack(owners, slots, exchange(outgoing), gradient.shape, capacity)

    def shared(send, sums, slots, info, left_away, right_away, gradient, left_set, rights):
        partner = [(i, i ^ 1) for i in range(group_size)]
        received, left_away, right_away = lax.optimization_barrier(
            (exchange(send), left_away, right_away)
        )
        own = received[:, full * row_count :, :]
        other = lax.ppermute(own, "dp", partner)
        left_away = lax.ppermute(left_away, "dp", partner)
        right_away = lax.ppermute(right_away, "dp", partner)
        outgoing, squares = multiply(
            info, sums, received, left_set, rights, full, full * slot_tiles + lane_tiles + 1, False,
        )
        outgoing = multiply_shared(
            info, sums, squares, own, other, left_set, rights, left_away, right_away, outgoing
        )
        return unpack(owners, slots, exchange(outgoing), gradient.shape, full)

    return lax.cond(
        conflict[0] > 0, general, shared,
        send, sums, slots, info, left_away, right_away, gradient, left_set, rights,
    )


def solution(mesh):
    return jax.shard_map(
        on_device,
        mesh=mesh,
        in_specs=(
            P(None, "dp", "mp"),
            P(None, "dp", "mp"),
            P(),
            P("dp", "mp", None, None, None),
            P("dp", "mp", None, None, None),
        ),
        out_specs=P(None, "dp", "mp"),
        check_vma=False,
    )
```

```python
import functools

import jax
import jax.numpy as jnp
from jax import lax
from jax.experimental import pallas as pl
from jax.experimental.pallas import tpu as pltpu
from jax.sharding import PartitionSpec as P

beta_two = 0.95
eps_adam = 1e-08
eps_norm = 1e-06

TILE = 256
LANES = 128
SUBLANES = 16
IN_VMEM = pl.BlockSpec(memory_space=pltpu.VMEM)
IN_SMEM = pl.BlockSpec(memory_space=pltpu.SMEM)
IN_ANY = pl.BlockSpec(memory_space=pl.ANY)


def keep_hbm(*values):
    return [pltpu.with_memory_space_constraint(value, pltpu.HBM) for value in values]


def keep_vmem(*values):
    return [pltpu.with_memory_space_constraint(value, pltpu.VMEM) for value in values]


def pack_kernel(
    full_slots, capacity, first_pass, me_ref, owner_ref, grad_ref, moment_ref, left_ref, right_ref,
    send_ref, sums_ref, slot_ref, info_ref, conflict_ref, left_away, right_away,
    counts, table, stage, moments, partial, stage_sems, away_sems,
):
    block_rows, row_count, width = grad_ref.shape
    group_size, _, block_size = send_ref.shape
    block_cols = width // block_size
    half = row_count // 2
    pairs = [(grad_ref, stage)] + ([(moment_ref, moments)] if first_pass else [])
    loads = [
        [
            pltpu.make_async_copy(source.at[r], target.at[r], stage_sems.at[i, r])
            for i, (source, target) in enumerate(pairs)
        ]
        for r in range(block_rows)
    ]
    for row in loads:
        for load in row:
            load.start()
    me = me_ref[0]
    core = lax.rem(me, 2)
    if first_pass:
        away = [
            pltpu.make_async_copy(left_ref.at[capacity - 1, :, 1 - core], left_away, away_sems.at[0]),
            pltpu.make_async_copy(right_ref.at[capacity - 1], right_away, away_sems.at[1]),
        ]
        for copy in away:
            copy.start()

    for index in range(group_size):
        counts[index] = 0
        for slot in range(capacity):
            table[index * capacity + slot] = -1
    conflict_ref[0] = 0
    partial[...] = jnp.zeros(partial.shape, jnp.float32)

    def block(r, c):
        b = r * block_cols + c
        owner = owner_ref[b]
        slot = counts[owner]
        counts[owner] = slot + 1
        slot_ref[b] = slot
        columns = pl.ds(pl.multiple_of(c * block_size, block_size), block_size)
        shared = slot >= full_slots
        for h in range(2):
            target = jnp.where(shared, owner - lax.rem(owner, 2) + h, owner)
            start = jnp.where(shared, full_slots * row_count, slot * row_count + h * half)
            send_ref[target, pl.ds(pl.multiple_of(start, half), half), :] = stage[
                r, h * half : (h + 1) * half, columns
            ]
        partner = owner + 1 - 2 * lax.rem(owner, 2)
        taken = table[partner * capacity + capacity - 1] >= 0
        conflict_ref[0] = conflict_ref[0] | (shared & taken).astype(jnp.int32)
        table[owner * capacity + slot] = b
        if first_pass:
            total = jnp.zeros((8, LANES), jnp.float32)
            for k in range(0, block_size, 2 * LANES):
                part = pl.ds(pl.multiple_of(c * block_size + k, 2 * LANES), 2 * LANES)
                wide = stage[r, :, part].astype(jnp.float32)
                moment = beta_two * moments[r, :, part].astype(jnp.float32) + (
                    (1.0 - beta_two) * wide * wide
                )
                direction = wide / (jnp.sqrt(moment) + eps_adam)
                value = jnp.sum((direction * direction).reshape(row_count // 8, 8, -1), axis=0)
                total = total + value[:, :LANES] + value[:, LANES:]
            partial[pl.ds(b, 1), :] = jnp.sum(total, axis=0, keepdims=True)

    for r in range(block_rows):
        for load in loads[r]:
            load.wait()
        for c in range(block_cols):
            block(r, c)

    for slot in range(capacity):
        info_ref[slot] = table[me * capacity + slot]
    info_ref[capacity] = table[(me + 1 - 2 * core) * capacity + capacity - 1]
    info_ref[capacity + 1] = core
    sums_ref[...] = lax.dot_general(
        jnp.ones((8, LANES), jnp.float32),
        partial[...],
        (((1,), (1,)), ((), ())),
        precision=lax.Precision.HIGHEST,
        preferred_element_type=jnp.float32,
    )[0:1]
    if first_pass:
        for copy in away:
            copy.wait()


def pack(me, owners, gradient, second_moment, left_set, rights, rows, full_slots):
    first_pass = second_moment is not None
    capacity, group_size, _, half, block_size = left_set.shape
    return pl.pallas_call(
        functools.partial(pack_kernel, full_slots, capacity, first_pass),
        out_shape=(
            pltpu.VMEM((group_size, rows, block_size), jnp.bfloat16),
            jax.ShapeDtypeStruct((1, LANES), jnp.float32),
            jax.ShapeDtypeStruct(owners.shape, jnp.int32),
            jax.ShapeDtypeStruct((capacity + 2,), jnp.int32),
            jax.ShapeDtypeStruct((1,), jnp.int32),
            pltpu.VMEM((group_size, half, block_size), jnp.bfloat16),
            pltpu.VMEM((block_size, block_size), jnp.bfloat16),
        ),
        in_specs=[IN_SMEM, IN_SMEM] + [IN_ANY] * 4,
        out_specs=(IN_VMEM, IN_VMEM, IN_SMEM, IN_SMEM, IN_SMEM, IN_VMEM, IN_VMEM),
        scratch_shapes=[
            pltpu.SMEM((group_size,), jnp.int32),
            pltpu.SMEM((group_size * capacity,), jnp.int32),
            pltpu.VMEM(gradient.shape, jnp.bfloat16),
            pltpu.VMEM(gradient.shape, jnp.bfloat16),
            pltpu.VMEM((LANES, LANES), jnp.float32),
            pltpu.SemaphoreType.DMA((2, gradient.shape[0])),
            pltpu.SemaphoreType.DMA((2,)),
        ],
        compiler_params=pltpu.CompilerParams(vmem_limit_bytes=24 * 2**20),
        cost_estimate=pl.CostEstimate(
            flops=10 * gradient.size, bytes_accessed=8 * gradient.size, transcendentals=2 * gradient.size
        ),
    )(
        me,
        owners,
        *keep_hbm(gradient, second_moment if first_pass else gradient, left_set, rights),
    )


def three_parts(value):
    high = value.astype(jnp.bfloat16)
    wide = high.astype(jnp.float32)
    rest = jnp.where(wide == value, 0.0, value - wide)
    middle = rest.astype(jnp.bfloat16)
    low = (rest - middle.astype(jnp.float32)).astype(jnp.bfloat16)
    return high, middle, low


def extra_tile(sums, squares, block_size):
    sums, squares = (value / float(block_size * block_size) for value in (sums, squares))
    rows = lax.broadcasted_iota(jnp.int32, (SUBLANES, LANES), 0)
    content = jnp.zeros((SUBLANES, LANES), jnp.float32)
    for i, part in enumerate([*three_parts(sums), *three_parts(squares)]):
        content = jnp.where(rows == i, part.astype(jnp.float32), content)
    return content.astype(jnp.bfloat16)


def block_product(left_rows, grad, right, times, put):
    count = times.shape[0] // TILE
    for m in range(count):
        times[m * TILE : (m + 1) * TILE, :] = jnp.dot(
            left_rows(m), grad(), preferred_element_type=jnp.float32
        ).astype(jnp.bfloat16)
    total = jnp.zeros((8, times.shape[1]), jnp.float32)
    for m in range(count):
        value = jnp.dot(
            times[m * TILE : (m + 1) * TILE, :], right(), preferred_element_type=jnp.float32
        )
        total = total + jnp.sum((value * value).reshape(TILE // 8, 8, -1), axis=0)
        put(m, value.astype(jnp.bfloat16))
    return jnp.sum(jnp.sum(total, axis=0, keepdims=True), axis=1, keepdims=True)


def multiply_kernel(
    slot_count, final, info_ref, sums_ref, recv_ref, left_ref, right_ref, out_ref, squares_ref, times
):
    _, group_size, row_halves, _, block_size = left_ref.shape
    row_count = row_halves * SUBLANES
    per_tile = TILE // row_count
    lane_tiles = block_size // LANES
    lane = lax.broadcasted_iota(jnp.int32, (1, LANES), 1)
    squares = jnp.zeros((1, LANES), jnp.float32)
    for s in range(slot_count):
        def compute(s=s):
            def put(m, tile):
                for j in range(lane_tiles):
                    part = tile[:, j * LANES : (j + 1) * LANES].reshape(
                        per_tile, row_halves, SUBLANES, LANES
                    )
                    for h in range(row_halves):
                        out_ref[
                            m * per_tile : (m + 1) * per_tile, (s * row_halves + h) * lane_tiles + j
                        ] = part[:, h]

            return block_product(
                lambda m: left_ref[s, m * per_tile : (m + 1) * per_tile].reshape(TILE, block_size),
                lambda: recv_ref[:, s * row_count : (s + 1) * row_count, :].reshape(
                    block_size, block_size
                ),
                lambda: right_ref[s],
                times,
                put,
            )

        value = lax.cond(info_ref[s] >= 0, compute, lambda: jnp.zeros((1, 1), jnp.float32))
        squares = squares + jnp.where(lane == info_ref[s], value, 0.0)
    squares_ref[...] = squares
    if final:
        out_ref[:, out_ref.shape[1] - 1] = jnp.broadcast_to(
            extra_tile(sums_ref[...], squares, block_size)[None], (group_size, SUBLANES, LANES)
        )


def multiply(info, sums, received, left_set, rights, slot_count, total_tiles, final):
    _, group_size, _, _, block_size = left_set.shape
    return pl.pallas_call(
        functools.partial(multiply_kernel, slot_count, final),
        out_shape=(
            pltpu.VMEM((group_size, total_tiles, SUBLANES, LANES), jnp.bfloat16),
            jax.ShapeDtypeStruct((1, LANES), jnp.float32),
        ),
        in_specs=[IN_SMEM] + [IN_VMEM] * 4,
        out_specs=(IN_VMEM, IN_VMEM),
        scratch_shapes=[pltpu.VMEM((block_size, block_size), jnp.bfloat16)],
        compiler_params=pltpu.CompilerParams(vmem_limit_bytes=12 * 2**20),
        cost_estimate=pl.CostEstimate(
            flops=slot_count * 4 * block_size**3,
            bytes_accessed=slot_count * 8 * block_size**2,
            transcendentals=0,
        ),
    )(info, sums, *keep_vmem(received, left_set, rights))


def shared_kernel(
    info_ref, sums_ref, squares_ref, own_ref, other_ref, left_ref, right_ref, left_away, right_away,
    before_ref, out_ref, grad, times,
):
    group_size, _, half, block_size = grad.shape
    per_tile = TILE // half
    lane_tiles = block_size // LANES
    first_tile = out_ref.shape[1] - 1 - lane_tiles
    capacity = info_ref.shape[0] - 2
    block = jnp.maximum(info_ref[capacity - 1], info_ref[capacity])
    core = info_ref[capacity + 1]
    del before_ref

    def compute(left_from, right_from):
        grad[:, pl.ds(core, 1)] = own_ref[...][:, None]
        grad[:, pl.ds(1 - core, 1)] = other_ref[...][:, None]

        def put(m, tile):
            for j in range(lane_tiles):
                out_ref[m * per_tile : (m + 1) * per_tile, first_tile + j] = tile[
                    :, j * LANES : (j + 1) * LANES
                ].reshape(per_tile, SUBLANES, LANES)

        return block_product(
            lambda m: left_from[m * per_tile : (m + 1) * per_tile].reshape(TILE, block_size),
            lambda: grad[...].reshape(block_size, block_size),
            lambda: right_from[...],
            times,
            put,
        )

    value = lax.cond(
        info_ref[capacity - 1] >= 0,
        lambda: compute(left_ref.at[capacity - 1, :, core], right_ref.at[capacity - 1]),
        lambda: lax.cond(
            block >= 0,
            lambda: compute(left_away, right_away),
            lambda: jnp.zeros((1, 1), jnp.float32),
        ),
    )
    lane = lax.broadcasted_iota(jnp.int32, (1, LANES), 1)
    squares = squares_ref[...] + jnp.where(lane == block, value, 0.0)
    out_ref[:, out_ref.shape[1] - 1] = jnp.broadcast_to(
        extra_tile(sums_ref[...], squares, block_size)[None], (group_size, SUBLANES, LANES)
    )


def multiply_shared(
    info, sums, squares, own, other, left_set, rights, left_away, right_away, outgoing
):
    group_size, half, block_size = own.shape
    rows = group_size * half
    return pl.pallas_call(
        shared_kernel,
        out_shape=pltpu.VMEM(outgoing.shape, outgoing.dtype),
        in_specs=[IN_SMEM] + [IN_VMEM] * 9,
        out_specs=IN_VMEM,
        input_output_aliases={9: 0},
        scratch_shapes=[
            pltpu.VMEM((group_size, 2, half, block_size), jnp.bfloat16),
            pltpu.VMEM((rows, block_size), jnp.bfloat16),
        ],
        compiler_params=pltpu.CompilerParams(vmem_limit_bytes=14 * 2**20),
        cost_estimate=pl.CostEstimate(
            flops=4 * rows * block_size**2, bytes_accessed=8 * rows * block_size, transcendentals=0
        ),
    )(
        info, sums, squares,
        *keep_vmem(own, other, left_set, rights, left_away, right_away, outgoing),
    )


def unpack_kernel(full_slots, owner_ref, slot_ref, back_ref, out_ref, stage, out_sems):
    block_rows, row_count, width = stage.shape
    block_count = owner_ref.shape[0]
    block_cols = block_count // block_rows
    block_size = width // block_cols
    row_halves = row_count // SUBLANES
    lane_tiles = block_size // LANES
    last = back_ref.shape[1] - 1
    found = jnp.sum(back_ref[:, last].astype(jnp.float32), axis=0)
    rms_adam = jnp.sqrt(found[0:1] + found[1:2] + found[2:3] + eps_norm)
    rms_shampoo = jnp.sqrt(found[3:4] + found[4:5] + found[5:6] + eps_norm)
    scale = rms_adam / rms_shampoo
    writes = []
    for r in range(block_rows):
        for c in range(block_cols):
            b = r * block_cols + c
            factor = jnp.broadcast_to(scale[:, b : b + 1], (SUBLANES, LANES))
            owner, slot = owner_ref[b], slot_ref[b]
            for h in range(row_halves):
                whole = slot < full_slots
                source = jnp.where(whole, owner, 2 * lax.div(owner, 2) + h)
                first = jnp.where(
                    whole, (slot * row_halves + h) * lane_tiles, full_slots * row_halves * lane_tiles
                )
                for j in range(lane_tiles):
                    stage[
                        r,
                        h * SUBLANES : (h + 1) * SUBLANES,
                        c * block_size + j * LANES : c * block_size + (j + 1) * LANES,
                    ] = (back_ref[source, first + j].astype(jnp.float32) * factor).astype(jnp.bfloat16)
        write = pltpu.make_async_copy(stage.at[r], out_ref.at[r], out_sems.at[r])
        write.start()
        writes.append(write)
    for write in writes:
        write.wait()


def unpack(owners, slots, back, shape, full_slots):
    block_rows, row_count, width = shape
    return pl.pallas_call(
        functools.partial(unpack_kernel, full_slots),
        out_shape=pltpu.HBM(shape, jnp.bfloat16),
        in_specs=[IN_SMEM, IN_SMEM, IN_VMEM],
        out_specs=IN_ANY,
        scratch_shapes=[
            pltpu.VMEM(shape, jnp.bfloat16),
            pltpu.SemaphoreType.DMA((block_rows,)),
        ],
        compiler_params=pltpu.CompilerParams(vmem_limit_bytes=32 * 2**20),
        cost_estimate=pl.CostEstimate(
            flops=block_rows * row_count * width,
            bytes_accessed=4 * block_rows * row_count * width,
            transcendentals=0,
        ),
    )(owners, slots, *keep_vmem(back))


def exchange(value):
    return lax.all_to_all(value, "dp", split_axis=0, concat_axis=0, tiled=True)


def on_device(gradient, second_moment, owner_table, left_roots, right_roots):
    group_size = lax.axis_size("dp")
    my_index = lax.axis_index("dp")
    _, row_count, width = gradient.shape
    block_size = left_roots.shape[-1]
    capacity = left_roots.shape[2]
    full = capacity - 1
    half = row_count // 2
    lane_tiles = block_size // LANES
    slot_tiles = lane_tiles * (row_count // SUBLANES)
    owners = owner_table[:, 0]
    me = my_index.reshape(1)
    left_set = left_roots.reshape(capacity, group_size, 2, half, block_size)
    rights = right_roots[0, 0]
    send, sums, slots, info, conflict, left_away, right_away = pack(
        me, owners, gradient, second_moment, left_set, rights, full * row_count + half, full
    )

    def general(send, sums, slots, info, left_away, right_away, gradient, left_set, rights):
        send = pack(
            me, owners, gradient, None, left_set, rights, capacity * row_count, capacity
        )[0]
        outgoing = multiply(
            info, sums, exchange(send), left_set, rights, capacity, capacity * slot_tiles + 1, True,
        )[0]
        return unpack(owners, slots, exchange(outgoing), gradient.shape, capacity)

    def shared(send, sums, slots, info, left_away, right_away, gradient, left_set, rights):
        partner = [(i, i ^ 1) for i in range(group_size)]
        received, left_away, right_away = lax.optimization_barrier(
            (exchange(send), left_away, right_away)
        )
        own = received[:, full * row_count :, :]
        other = lax.ppermute(own, "dp", partner)
        left_away = lax.ppermute(left_away, "dp", partner)
        right_away = lax.ppermute(right_away, "dp", partner)
        outgoing, squares = multiply(
            info, sums, received, left_set, rights, full, full * slot_tiles + lane_tiles + 1, False,
        )
        outgoing = multiply_shared(
            info, sums, squares, own, other, left_set, rights, left_away, right_away, outgoing
        )
        return unpack(owners, slots, exchange(outgoing), gradient.shape, full)

    return lax.cond(
        conflict[0] > 0, general, shared,
        send, sums, slots, info, left_away, right_away, gradient, left_set, rights,
    )


def solution(mesh):
    return jax.shard_map(
        on_device,
        mesh=mesh,
        in_specs=(
            P(None, "dp", "mp"),
            P(None, "dp", "mp"),
            P(),
            P("dp", "mp", None, None, None),
            P("dp", "mp", None, None, None),
        ),
        out_specs=P(None, "dp", "mp"),
        check_vma=False,
    )
```

```python
import functools

import jax
import jax.numpy as jnp
from jax import lax
from jax.experimental import pallas as pl
from jax.experimental.pallas import tpu as pltpu
from jax.sharding import PartitionSpec as P

beta_two = 0.95
eps_adam = 1e-08
eps_norm = 1e-06

TILE = 512
LANES = 128
SUBLANES = 16
IN_VMEM = pl.BlockSpec(memory_space=pltpu.VMEM)
IN_SMEM = pl.BlockSpec(memory_space=pltpu.SMEM)
IN_ANY = pl.BlockSpec(memory_space=pl.ANY)


def keep_hbm(*values):
    return [pltpu.with_memory_space_constraint(value, pltpu.HBM) for value in values]


def keep_vmem(*values):
    return [pltpu.with_memory_space_constraint(value, pltpu.VMEM) for value in values]


def pack_kernel(
    full_slots, capacity, first_pass, me_ref, owner_ref, grad_ref, moment_ref, left_ref, right_ref,
    send_ref, sums_ref, slot_ref, info_ref, conflict_ref, left_away, right_away,
    counts, table, stage, moments, partial, stage_sems, away_sems,
):
    block_rows, row_count, width = grad_ref.shape
    group_size, _, block_size = send_ref.shape
    block_cols = width // block_size
    half = row_count // 2
    pairs = [(grad_ref, stage)] + ([(moment_ref, moments)] if first_pass else [])
    loads = [
        [
            pltpu.make_async_copy(source.at[r], target.at[r], stage_sems.at[i, r])
            for i, (source, target) in enumerate(pairs)
        ]
        for r in range(block_rows)
    ]
    for row in loads:
        for load in row:
            load.start()
    me = me_ref[0]
    core = lax.rem(me, 2)
    if first_pass:
        away = [
            pltpu.make_async_copy(left_ref.at[capacity - 1, :, 1 - core], left_away, away_sems.at[0]),
            pltpu.make_async_copy(right_ref.at[capacity - 1], right_away, away_sems.at[1]),
        ]

    for index in range(group_size):
        counts[index] = 0
        for slot in range(capacity):
            table[index * capacity + slot] = -1
    conflict_ref[0] = 0
    partial[...] = jnp.zeros(partial.shape, jnp.float32)

    def block(r, c):
        b = r * block_cols + c
        owner = owner_ref[b]
        slot = counts[owner]
        counts[owner] = slot + 1
        slot_ref[b] = slot
        columns = pl.ds(pl.multiple_of(c * block_size, block_size), block_size)
        shared = slot >= full_slots
        for h in range(2):
            target = jnp.where(shared, owner - lax.rem(owner, 2) + h, owner)
            start = jnp.where(shared, full_slots * row_count, slot * row_count + h * half)
            send_ref[target, pl.ds(pl.multiple_of(start, half), half), :] = stage[
                r, h * half : (h + 1) * half, columns
            ]
        partner = owner + 1 - 2 * lax.rem(owner, 2)
        taken = table[partner * capacity + capacity - 1] >= 0
        conflict_ref[0] = conflict_ref[0] | (shared & taken).astype(jnp.int32)
        table[owner * capacity + slot] = b
        if first_pass:
            total = jnp.zeros((8, LANES), jnp.float32)
            for k in range(0, block_size, 2 * LANES):
                part = pl.ds(pl.multiple_of(c * block_size + k, 2 * LANES), 2 * LANES)
                wide = stage[r, :, part].astype(jnp.float32)
                moment = beta_two * moments[r, :, part].astype(jnp.float32) + (
                    (1.0 - beta_two) * wide * wide
                )
                direction = wide / (jnp.sqrt(moment) + eps_adam)
                value = jnp.sum((direction * direction).reshape(row_count // 8, 8, -1), axis=0)
                total = total + value[:, :LANES] + value[:, LANES:]
            partial[pl.ds(b, 1), :] = jnp.sum(total, axis=0, keepdims=True)

    for r in range(block_rows):
        for load in loads[r]:
            load.wait()
        if first_pass and r == block_rows // 2:
            for copy in away:
                copy.start()
        for c in range(block_cols):
            block(r, c)

    for slot in range(capacity):
        info_ref[slot] = table[me * capacity + slot]
    info_ref[capacity] = table[(me + 1 - 2 * core) * capacity + capacity - 1]
    info_ref[capacity + 1] = core
    sums_ref[...] = lax.dot_general(
        jnp.ones((8, LANES), jnp.float32),
        partial[...],
        (((1,), (1,)), ((), ())),
        precision=lax.Precision.HIGHEST,
        preferred_element_type=jnp.float32,
    )[0:1]
    if first_pass:
        for copy in away:
            copy.wait()


def pack(me, owners, gradient, second_moment, left_set, rights, rows, full_slots):
    first_pass = second_moment is not None
    capacity, group_size, _, half, block_size = left_set.shape
    return pl.pallas_call(
        functools.partial(pack_kernel, full_slots, capacity, first_pass),
        out_shape=(
            pltpu.VMEM((group_size, rows, block_size), jnp.bfloat16),
            jax.ShapeDtypeStruct((1, LANES), jnp.float32),
            jax.ShapeDtypeStruct(owners.shape, jnp.int32),
            jax.ShapeDtypeStruct((capacity + 2,), jnp.int32),
            jax.ShapeDtypeStruct((1,), jnp.int32),
            pltpu.VMEM((group_size, half, block_size), jnp.bfloat16),
            pltpu.VMEM((block_size, block_size), jnp.bfloat16),
        ),
        in_specs=[IN_SMEM, IN_SMEM] + [IN_ANY] * 4,
        out_specs=(IN_VMEM, IN_VMEM, IN_SMEM, IN_SMEM, IN_SMEM, IN_VMEM, IN_VMEM),
        scratch_shapes=[
            pltpu.SMEM((group_size,), jnp.int32),
            pltpu.SMEM((group_size * capacity,), jnp.int32),
            pltpu.VMEM(gradient.shape, jnp.bfloat16),
            pltpu.VMEM(gradient.shape, jnp.bfloat16),
            pltpu.VMEM((LANES, LANES), jnp.float32),
            pltpu.SemaphoreType.DMA((2, gradient.shape[0])),
            pltpu.SemaphoreType.DMA((2,)),
        ],
        compiler_params=pltpu.CompilerParams(vmem_limit_bytes=24 * 2**20),
        cost_estimate=pl.CostEstimate(
            flops=10 * gradient.size, bytes_accessed=8 * gradient.size, transcendentals=2 * gradient.size
        ),
    )(
        me,
        owners,
        *keep_hbm(gradient, second_moment if first_pass else gradient, left_set, rights),
    )


def three_parts(value):
    high = value.astype(jnp.bfloat16)
    wide = high.astype(jnp.float32)
    rest = jnp.where(wide == value, 0.0, value - wide)
    middle = rest.astype(jnp.bfloat16)
    low = (rest - middle.astype(jnp.float32)).astype(jnp.bfloat16)
    return high, middle, low


def extra_tile(sums, squares, block_size):
    sums, squares = (value / float(block_size * block_size) for value in (sums, squares))
    rows = lax.broadcasted_iota(jnp.int32, (SUBLANES, LANES), 0)
    content = jnp.zeros((SUBLANES, LANES), jnp.float32)
    for i, part in enumerate([*three_parts(sums), *three_parts(squares)]):
        content = jnp.where(rows == i, part.astype(jnp.float32), content)
    return content.astype(jnp.bfloat16)


def block_product(left_rows, grad, right, times, put):
    count = times.shape[0] // TILE
    for m in range(count):
        times[m * TILE : (m + 1) * TILE, :] = jnp.dot(
            left_rows(m), grad(), preferred_element_type=jnp.float32
        ).astype(jnp.bfloat16)
    total = jnp.zeros((8, times.shape[1]), jnp.float32)
    for m in range(count):
        value = jnp.dot(
            times[m * TILE : (m + 1) * TILE, :], right(), preferred_element_type=jnp.float32
        )
        total = total + jnp.sum((value * value).reshape(TILE // 8, 8, -1), axis=0)
        put(m, value.astype(jnp.bfloat16))
    return jnp.sum(jnp.sum(total, axis=0, keepdims=True), axis=1, keepdims=True)


def multiply_kernel(
    slot_count, final, info_ref, sums_ref, recv_ref, left_ref, right_ref, out_ref, squares_ref, times
):
    _, group_size, row_halves, _, block_size = left_ref.shape
    row_count = row_halves * SUBLANES
    per_tile = TILE // row_count
    lane_tiles = block_size // LANES
    lane = lax.broadcasted_iota(jnp.int32, (1, LANES), 1)
    squares = jnp.zeros((1, LANES), jnp.float32)
    for s in range(slot_count):
        def compute(s=s):
            def put(m, tile):
                for j in range(lane_tiles):
                    part = tile[:, j * LANES : (j + 1) * LANES].reshape(
                        per_tile, row_halves, SUBLANES, LANES
                    )
                    for h in range(row_halves):
                        out_ref[
                            m * per_tile : (m + 1) * per_tile, (s * row_halves + h) * lane_tiles + j
                        ] = part[:, h]

            return block_product(
                lambda m: left_ref[s, m * per_tile : (m + 1) * per_tile].reshape(TILE, block_size),
                lambda: recv_ref[:, s * row_count : (s + 1) * row_count, :].reshape(
                    block_size, block_size
                ),
                lambda: right_ref[s],
                times,
                put,
            )

        value = lax.cond(info_ref[s] >= 0, compute, lambda: jnp.zeros((1, 1), jnp.float32))
        squares = squares + jnp.where(lane == info_ref[s], value, 0.0)
    squares_ref[...] = squares
    if final:
        out_ref[:, out_ref.shape[1] - 1] = jnp.broadcast_to(
            extra_tile(sums_ref[...], squares, block_size)[None], (group_size, SUBLANES, LANES)
        )


def multiply(info, sums, received, left_set, rights, slot_count, total_tiles, final):
    _, group_size, _, _, block_size = left_set.shape
    return pl.pallas_call(
        functools.partial(multiply_kernel, slot_count, final),
        out_shape=(
            pltpu.VMEM((group_size, total_tiles, SUBLANES, LANES), jnp.bfloat16),
            jax.ShapeDtypeStruct((1, LANES), jnp.float32),
        ),
        in_specs=[IN_SMEM] + [IN_VMEM] * 4,
        out_specs=(IN_VMEM, IN_VMEM),
        scratch_shapes=[pltpu.VMEM((block_size, block_size), jnp.bfloat16)],
        compiler_params=pltpu.CompilerParams(vmem_limit_bytes=12 * 2**20),
        cost_estimate=pl.CostEstimate(
            flops=slot_count * 4 * block_size**3,
            bytes_accessed=slot_count * 8 * block_size**2,
            transcendentals=0,
        ),
    )(info, sums, *keep_vmem(received, left_set, rights))


def shared_kernel(
    info_ref, sums_ref, squares_ref, own_ref, other_ref, left_ref, right_ref, left_away, right_away,
    before_ref, out_ref, grad, times,
):
    group_size, _, half, block_size = grad.shape
    per_tile = TILE // half
    lane_tiles = block_size // LANES
    first_tile = out_ref.shape[1] - 1 - lane_tiles
    capacity = info_ref.shape[0] - 2
    block = jnp.maximum(info_ref[capacity - 1], info_ref[capacity])
    core = info_ref[capacity + 1]
    del before_ref

    def compute(left_from, right_from):
        grad[:, pl.ds(core, 1)] = own_ref[...][:, None]
        grad[:, pl.ds(1 - core, 1)] = other_ref[...][:, None]

        def put(m, tile):
            for j in range(lane_tiles):
                out_ref[m * per_tile : (m + 1) * per_tile, first_tile + j] = tile[
                    :, j * LANES : (j + 1) * LANES
                ].reshape(per_tile, SUBLANES, LANES)

        return block_product(
            lambda m: left_from[m * per_tile : (m + 1) * per_tile].reshape(TILE, block_size),
            lambda: grad[...].reshape(block_size, block_size),
            lambda: right_from[...],
            times,
            put,
        )

    value = lax.cond(
        info_ref[capacity - 1] >= 0,
        lambda: compute(left_ref.at[capacity - 1, :, core], right_ref.at[capacity - 1]),
        lambda: lax.cond(
            block >= 0,
            lambda: compute(left_away, right_away),
            lambda: jnp.zeros((1, 1), jnp.float32),
        ),
    )
    lane = lax.broadcasted_iota(jnp.int32, (1, LANES), 1)
    squares = squares_ref[...] + jnp.where(lane == block, value, 0.0)
    out_ref[:, out_ref.shape[1] - 1] = jnp.broadcast_to(
        extra_tile(sums_ref[...], squares, block_size)[None], (group_size, SUBLANES, LANES)
    )


def multiply_shared(
    info, sums, squares, own, other, left_set, rights, left_away, right_away, outgoing
):
    group_size, half, block_size = own.shape
    rows = group_size * half
    return pl.pallas_call(
        shared_kernel,
        out_shape=pltpu.VMEM(outgoing.shape, outgoing.dtype),
        in_specs=[IN_SMEM] + [IN_VMEM] * 9,
        out_specs=IN_VMEM,
        input_output_aliases={9: 0},
        scratch_shapes=[
            pltpu.VMEM((group_size, 2, half, block_size), jnp.bfloat16),
            pltpu.VMEM((rows, block_size), jnp.bfloat16),
        ],
        compiler_params=pltpu.CompilerParams(vmem_limit_bytes=14 * 2**20),
        cost_estimate=pl.CostEstimate(
            flops=4 * rows * block_size**2, bytes_accessed=8 * rows * block_size, transcendentals=0
        ),
    )(
        info, sums, squares,
        *keep_vmem(own, other, left_set, rights, left_away, right_away, outgoing),
    )


def unpack_kernel(full_slots, owner_ref, slot_ref, back_ref, out_ref, stage, out_sems):
    block_rows, row_count, width = stage.shape
    block_count = owner_ref.shape[0]
    block_cols = block_count // block_rows
    block_size = width // block_cols
    row_halves = row_count // SUBLANES
    lane_tiles = block_size // LANES
    last = back_ref.shape[1] - 1
    found = jnp.sum(back_ref[:, last].astype(jnp.float32), axis=0)
    rms_adam = jnp.sqrt(found[0:1] + found[1:2] + found[2:3] + eps_norm)
    rms_shampoo = jnp.sqrt(found[3:4] + found[4:5] + found[5:6] + eps_norm)
    scale = rms_adam / rms_shampoo
    writes = []
    for r in range(block_rows):
        for c in range(block_cols):
            b = r * block_cols + c
            factor = jnp.broadcast_to(scale[:, b : b + 1], (SUBLANES, LANES))
            owner, slot = owner_ref[b], slot_ref[b]
            for h in range(row_halves):
                whole = slot < full_slots
                source = jnp.where(whole, owner, 2 * lax.div(owner, 2) + h)
                first = jnp.where(
                    whole, (slot * row_halves + h) * lane_tiles, full_slots * row_halves * lane_tiles
                )
                for j in range(lane_tiles):
                    stage[
                        r,
                        h * SUBLANES : (h + 1) * SUBLANES,
                        c * block_size + j * LANES : c * block_size + (j + 1) * LANES,
                    ] = (back_ref[source, first + j].astype(jnp.float32) * factor).astype(jnp.bfloat16)
        write = pltpu.make_async_copy(stage.at[r], out_ref.at[r], out_sems.at[r])
        write.start()
        writes.append(write)
    for write in writes:
        write.wait()


def unpack(owners, slots, back, shape, full_slots):
    block_rows, row_count, width = shape
    return pl.pallas_call(
        functools.partial(unpack_kernel, full_slots),
        out_shape=pltpu.HBM(shape, jnp.bfloat16),
        in_specs=[IN_SMEM, IN_SMEM, IN_VMEM],
        out_specs=IN_ANY,
        scratch_shapes=[
            pltpu.VMEM(shape, jnp.bfloat16),
            pltpu.SemaphoreType.DMA((block_rows,)),
        ],
        compiler_params=pltpu.CompilerParams(vmem_limit_bytes=32 * 2**20),
        cost_estimate=pl.CostEstimate(
            flops=block_rows * row_count * width,
            bytes_accessed=4 * block_rows * row_count * width,
            transcendentals=0,
        ),
    )(owners, slots, *keep_vmem(back))


def exchange(value):
    return lax.all_to_all(value, "dp", split_axis=0, concat_axis=0, tiled=True)


def on_device(gradient, second_moment, owner_table, left_roots, right_roots):
    group_size = lax.axis_size("dp")
    my_index = lax.axis_index("dp")
    _, row_count, width = gradient.shape
    block_size = left_roots.shape[-1]
    capacity = left_roots.shape[2]
    full = capacity - 1
    half = row_count // 2
    lane_tiles = block_size // LANES
    slot_tiles = lane_tiles * (row_count // SUBLANES)
    owners = owner_table[:, 0]
    me = my_index.reshape(1)
    left_set = left_roots.reshape(capacity, group_size, 2, half, block_size)
    rights = right_roots[0, 0]
    send, sums, slots, info, conflict, left_away, right_away = pack(
        me, owners, gradient, second_moment, left_set, rights, full * row_count + half, full
    )

    def general(send, sums, slots, info, left_away, right_away, gradient, left_set, rights):
        send = pack(
            me, owners, gradient, None, left_set, rights, capacity * row_count, capacity
        )[0]
        outgoing = multiply(
            info, sums, exchange(send), left_set, rights, capacity, capacity * slot_tiles + 1, True,
        )[0]
        return unpack(owners, slots, exchange(outgoing), gradient.shape, capacity)

    def shared(send, sums, slots, info, left_away, right_away, gradient, left_set, rights):
        partner = [(i, i ^ 1) for i in range(group_size)]
        received, left_away, right_away = lax.optimization_barrier(
            (exchange(send), left_away, right_away)
        )
        own = received[:, full * row_count :, :]
        other = lax.ppermute(own, "dp", partner)
        left_away = lax.ppermute(left_away, "dp", partner)
        right_away = lax.ppermute(right_away, "dp", partner)
        outgoing, squares = multiply(
            info, sums, received, left_set, rights, full, full * slot_tiles + lane_tiles + 1, False,
        )
        outgoing = multiply_shared(
            info, sums, squares, own, other, left_set, rights, left_away, right_away, outgoing
        )
        return unpack(owners, slots, exchange(outgoing), gradient.shape, full)

    return lax.cond(
        conflict[0] > 0, general, shared,
        send, sums, slots, info, left_away, right_away, gradient, left_set, rights,
    )


def solution(mesh):
    return jax.shard_map(
        on_device,
        mesh=mesh,
        in_specs=(
            P(None, "dp", "mp"),
            P(None, "dp", "mp"),
            P(),
            P("dp", "mp", None, None, None),
            P("dp", "mp", None, None, None),
        ),
        out_specs=P(None, "dp", "mp"),
        check_vma=False,
    )
```
